32 devices in a mesh: freq: 4 (over x, core), sky: 8 (over z, y).
Axes of the slice: x: 2, y: 2, z: 4, core: 2. Of those that a mesh axis runs over, the one named last changes fastest.
Arguments:
- sky_cube: bfloat16 [16, 256, 1024], P('freq', 'sky'), may hold values from -6 to 6
- half_width: int32 [16], P('freq'), may hold values from 2 to 12, as said below
- conv_weight: bfloat16 [16, 27], replicated, may hold values from -0.3125 to 0.3125
- out_cotangent: bfloat16 [16, 16, 256, 1024], P(None, 'freq', 'sky'), may hold values from -6 to 6
Outputs:
- sky_grad: float32 [16, 256, 1024], P('freq', 'sky')
- kernel_grad: float32 [16, 27], replicated
The draws below stay inside these ranges and needn't reach their ends.
Inputs may be any that keep to these rules, and one draw needn't show every extreme that they name: half_width[f] differs by at most one from 2 + floor((10) (15 - f) / 15); the first frequency has exactly 12 and the last exactly 2.
All inputs are finite; a program needn't handle non-finite values.
Results may differ from the reference program's by a relative error of at most 0.0033.
Values may be sent and summed in bfloat16 or wider, within the bound.
A program may use at most 128 MiB of HBM per device.

```python
import math
import jax
import jax.numpy as jnp
from jax import lax

V = 1024
CH = 16
TAPS = 27
MAXH = 12
FREQS = 16
U = 256


def draw_half_width(key, part):
    freq_index = jnp.arange(FREQS, dtype=jnp.int32)
    base_width = 2 + (MAXH - 2) * (FREQS - 1 - freq_index) // (FREQS - 1)
    jitter = jax.random.randint(key, (FREQS,), -1, 2, dtype=jnp.int32)
    widths = jnp.clip(base_width + jitter, 2, MAXH)
    widths = widths.at[0].set(MAXH).at[FREQS - 1].set(2)
    return widths.astype(jnp.int32)


def block_levels(key, shape, cuts, low, largest):
    factor_of = 1.0
    for position, shards_of in cuts:
        draws = jax.random.uniform(jax.random.fold_in(jax.random.fold_in(key, 6), position), (shards_of,), jnp.float32, low / len(cuts), largest / len(cuts))
        factor_of = factor_of * jnp.repeat(jnp.exp(draws), shape[position] // shards_of).reshape((-1,) + (1,) * (len(shape) - 1 - position))
    return factor_of


def gaussian(rng, dims, width, bound, pieces=(), held_as=jnp.bfloat16):
    array = width * jax.random.normal(rng, dims, jnp.float32)
    if pieces:
        array = array * block_levels(rng, dims, pieces, -0.22, 0.18)
    return jnp.clip(array, -bound, bound).astype(held_as)


def setup_inputs(seed: int = 0) -> dict:
    splits = jax.random.split(jax.random.key(seed), 5)
    return {
        "sky_cube": gaussian(splits[0], (FREQS, U, V), 1.0, 6.0, ((0, 4), (1, 8))),
        "half_width": draw_half_width(jax.random.fold_in(splits[4], 71), 0),
        "conv_weight": gaussian(splits[2], (CH, TAPS), (CH * TAPS) ** -0.5, 0.3125),
        "out_cotangent": gaussian(splits[3], (CH, FREQS, U, V), 1.0, 6.0, ((1, 4), (2, 8))),
    }


def beam_taps(half_width):
    offsets = jnp.arange(-MAXH, MAXH + 1, dtype=jnp.int32)
    inside = jnp.abs(offsets)[None, :] <= half_width[:, None]
    spread = half_width.astype(jnp.float32)[:, None]
    offset_sq = (offsets.astype(jnp.float32) ** 2)[None, :]
    profile = jnp.where(inside, jnp.exp(-2.0 * offset_sq / (spread * spread)), jnp.float32(0.0))
    return profile / jnp.sqrt(lax.optimization_barrier(jnp.sum(profile * profile, axis=1, keepdims=True)))

def blur_columns(source, kernel_taps):
    length = source.shape[2]
    padded = jnp.pad(source, ((0, 0), (0, 0), (MAXH, MAXH)))
    summed = jnp.zeros_like(source)
    for j in range(2 * MAXH + 1):
        summed = summed + kernel_taps[:, j][:, None, None] * padded[:, :, j:j + length]
    return summed

def blur_rows(source, kernel_taps):
    length = source.shape[1]
    padded = jnp.pad(source, ((0, 0), (MAXH, MAXH), (0, 0)))
    summed = jnp.zeros_like(source)
    for j in range(2 * MAXH + 1):
        summed = summed + kernel_taps[:, j][:, None, None] * padded[:, j:j + length, :]
    return summed

def reference(sky_cube, half_width, conv_weight, out_cotangent):
    kernel_taps = beam_taps(half_width)
    beam_field = blur_rows(blur_columns(sky_cube.astype(jnp.float32), kernel_taps), kernel_taps).astype(jnp.bfloat16)
    framed = jnp.pad(beam_field, 1)
    cot_pad = jnp.pad(out_cotangent, ((0, 0), (1, 1), (1, 1), (1, 1)))
    weights = conv_weight.astype(jnp.float32)
    row_count = beam_field.shape[1]
    col_count = beam_field.shape[2]

    def plane_terms(plane_index):
        cot_plane = lax.dynamic_index_in_dim(out_cotangent, plane_index, 1, keepdims=False).astype(jnp.float32)
        beam_block = lax.dynamic_slice_in_dim(framed, plane_index, 3, 0).astype(jnp.float32)
        cot_block = lax.dynamic_slice_in_dim(cot_pad, plane_index, 3, 1).astype(jnp.float32)
        grad_terms = []
        back_plane = jnp.zeros((row_count, col_count), jnp.float32)
        for a in range(3):
            for b in range(3):
                for e in range(3):
                    shifted = beam_block[a, b:b + row_count, e:e + col_count]
                    grad_terms.append(jnp.einsum('cuv,uv->c', cot_plane, shifted))
                    moved = cot_block[:, 2 - a, 2 - b:2 - b + row_count, 2 - e:2 - e + col_count]
                    back_plane = back_plane + jnp.einsum('c,cuv->uv', weights[:, 9 * a + 3 * b + e], moved)
        return (jnp.stack(grad_terms, axis=1), back_plane)
    grad_terms, back_planes = lax.map(plane_terms, jnp.arange(beam_field.shape[0], dtype=jnp.int32))
    kernel_grad = lax.optimization_barrier(jnp.sum(grad_terms, axis=0)) * (1.0 / math.sqrt(FREQS * U * V))
    grad_beam = back_planes.astype(jnp.bfloat16)
    sky_grad = blur_rows(blur_columns(grad_beam.astype(jnp.float32), kernel_taps), kernel_taps)
    return (sky_grad, kernel_grad)
```

```python
import math

import jax
import jax.numpy as jnp
from jax import lax
from jax.experimental import pallas as pl
from jax.experimental.pallas import tpu as pltpu
from jax.sharding import PartitionSpec as P

MAXH = 12
HALO = 16
PAD = 128
BLOCK = 128
EDGE = 40
BROWS = 48
F32 = jnp.float32
BF16 = jnp.bfloat16
MESH = pl.DeviceIdType.MESH
DIRS = [(df, ds) for df in (-1, 0, 1) for ds in (-1, 0, 1) if (df, ds) != (0, 0)]


def iota(shape, dim):
    return lax.broadcasted_iota(jnp.int32, shape, dim)


def row_of(r, rows):
    return jnp.where(r <= rows, r, jnp.where(r == rows + 1, -1, -1000))


def band_mask(b, height, rows, width):
    shape = (height, width)
    return row_of(iota(shape, 0), rows) == lax.rem(iota(shape, 1), rows) + (b - 1)


def shift_next(x):
    n = x.shape[-1]
    return jnp.where(iota(x.shape, 1) == n - 1, 0.0, pltpu.roll(x, n - 1, 1))


def shift_prev(x):
    n = x.shape[-1]
    return jnp.where(iota(x.shape, 1) == 0, 0.0, pltpu.roll(x, 1, 1))


def body(nf, ns, scale, hw_ref, sky_ref, w_ref, cot_ref, out_ref, kg_ref,
         skyh, gbh, cotv, bmat, acc, part, eu, ed, pf, pe, bs, tcol, trow, hwb,
         mine, slots, mine2, slots2,
         cot_sem, own_sem, s_sky, r_sky, s_hw, r_hw, s_part, r_part, s_gb, r_gb,
         s_kg, r_kg, s_kf, r_kf):
    planes, rows, length = out_ref.shape
    chans = w_ref.shape[0]
    wide = chans * rows
    tall = rows + 2 * HALO
    fi, si = lax.axis_index("freq"), lax.axis_index("sky")

    def valid(df, ds):
        ok = None
        for at, step, size in ((fi, df, nf), (si, ds, ns)):
            if step:
                one = at + step < size if step > 0 else at + step >= 0
                ok = one if ok is None else jnp.logical_and(ok, one)
        return ok

    def span(step, own_lo, own_n, halo_n, full_n):
        if step == 0:
            return own_lo, 0, own_n
        if step > 0:
            return own_lo - halo_n, own_n - halo_n, halo_n
        return own_lo + own_n, 0, halo_n

    lanes = pl.ds(PAD, length)

    cot_copies = [pltpu.make_async_copy(cot_ref.at[:, g], cotv.at[g], cot_sem.at[g])
                  for g in range(planes)]
    for copy in cot_copies:
        copy.start()
    own = pltpu.make_async_copy(
        sky_ref, skyh.at[pl.ds(1, planes), pl.ds(HALO, rows), lanes], own_sem.at[0])
    own.start()
    for ref in (skyh, gbh):
        n = ref.shape[0]
        ref[:, :, 0:PAD] = jnp.zeros((n, tall, PAD), BF16)
        ref[:, :, PAD + length:] = jnp.zeros((n, tall, PAD), BF16)
    for k in range(planes):
        hwb[1 + k] = jnp.full((8, 256), hw_ref[k].astype(F32))

    def dst_sky(df, ds):
        p0, _, pn = span(df, 1, planes, 1, planes + 2)
        r0, _, rn = span(ds, HALO, rows, HALO, tall)
        return skyh.at[pl.ds(p0, pn), pl.ds(r0, rn), lanes]

    for i, (df, ds) in enumerate(DIRS):
        @pl.when(jnp.logical_not(valid(-df, -ds)))
        def _(df=df, ds=ds):
            ref = dst_sky(df, ds)
            ref[...] = jnp.zeros(ref.shape, BF16)
            if df == 0:
                r0, _, rn = span(ds, HALO, rows, HALO, tall)
                gbh[:, r0:r0 + rn, PAD:PAD + length] = jnp.zeros((planes, rn, length), BF16)
            if ds == 0:
                hwb[0 if df > 0 else planes + 1] = jnp.ones((8, 256), F32)
                pf[0 if df > 0 else 1] = jnp.zeros((rows, length), F32)
            else:
                pe[(df + 1) * 2 + (ds > 0)] = jnp.zeros((8, length), F32)

    barrier = pltpu.get_barrier_semaphore()
    for k in range(1, ns):
        pl.semaphore_signal(barrier, inc=1, device_id=(fi, lax.rem(si + k, ns)), device_id_type=MESH)
    for k in range(1, nf):
        pl.semaphore_signal(barrier, inc=1, device_id=(lax.rem(fi + k, nf), si), device_id_type=MESH)
    greeted = jnp.int32(ns + nf - 2)
    for df, ds in DIRS:
        if df and ds:
            ok = valid(df, ds)
            greeted = greeted + jnp.where(ok, 1, 0)

            @pl.when(ok)
            def _(df=df, ds=ds):
                pl.semaphore_signal(barrier, inc=1, device_id=(fi + df, si + ds), device_id_type=MESH)

    pl.semaphore_wait(barrier, greeted)

    def remote(src, dst, send, recv, df, ds):
        return pltpu.make_async_remote_copy(
            src_ref=src, dst_ref=dst, send_sem=send, recv_sem=recv,
            device_id=(fi + df, si + ds), device_id_type=MESH)

    def sky_copy(i, df, ds):
        _, p0, pn = span(df, 1, planes, 1, planes + 2)
        _, r0, rn = span(ds, HALO, rows, HALO, tall)
        return remote(sky_ref.at[pl.ds(p0, pn), pl.ds(r0, rn), :], dst_sky(df, ds),
                      s_sky.at[i], r_sky.at[i], df, ds)

    def hw_copy(df):
        j = 0 if df > 0 else 1
        return remote(hwb.at[planes if df > 0 else 1], hwb.at[0 if df > 0 else planes + 1],
                      s_hw.at[j], r_hw.at[j], df, 0)

    def part_copy(i, df, ds):
        if ds == 0:
            src, dst = part.at[planes + 1 if df > 0 else 0, pl.ds(0, rows)], pf.at[0 if df > 0 else 1]
        else:
            src, dst = (ed if ds > 0 else eu), pe.at[(df + 1) * 2 + (ds > 0)]
        return remote(src, dst, s_part.at[i], r_part.at[i], df, ds)

    def gb_copy(ds):
        j = 0 if ds > 0 else 1
        r0, r1, rn = span(ds, HALO, rows, HALO, tall)
        return remote(gbh.at[:, pl.ds(HALO + r1, rn), :], gbh.at[:, pl.ds(r0, rn), :],
                      s_gb.at[j], r_gb.at[j], 0, ds)

    for i, (df, ds) in enumerate(DIRS):
        @pl.when(valid(df, ds))
        def _(i=i, df=df, ds=ds):
            sky_copy(i, df, ds).start()
            if ds == 0:
                hw_copy(df).start()

    member = (lax.div(iota((chans, wide), 1), rows) == iota((chans, wide), 0))
    spread = lax.dot_general(w_ref[...], member.astype(BF16), (((0,), (0,)), ((), ())),
                             preferred_element_type=F32)
    masks = [band_mask(b, EDGE, rows, wide) for b in range(3)]
    for a in range(3):
        for e in range(3):
            tile = jnp.zeros((EDGE, wide), F32)
            for b in range(3):
                k = 9 * a + 3 * b + e
                tile = tile + jnp.where(masks[b], spread[k:k + 1, :], 0.0)
            bmat[pl.ds((3 * a + e) * EDGE, EDGE), :] = tile
    acc[...] = jnp.zeros(acc.shape, F32)

    def project(g, carry):
        pltpu.make_async_copy(cot_ref.at[:, g], cotv.at[g], cot_sem.at[g]).wait()
        res = jnp.dot(bmat[...].astype(BF16), cotv[g].reshape(wide, length),
                      preferred_element_type=F32)
        acc[pl.ds(g, 3)] += res.reshape(3, 3, EDGE, length)
        return carry

    lax.fori_loop(0, planes, project, 0)
    for p in range(planes + 2):
        total = acc[p, 1] + shift_next(acc[p, 0]) + shift_prev(acc[p, 2])
        part[p] = total
        ed[p:p + 1, :] = total[rows:rows + 1]
        eu[p:p + 1, :] = total[rows + 1:rows + 2]
    eu[planes + 2:, :] = jnp.zeros((8 - planes - 2, length), F32)
    ed[planes + 2:, :] = jnp.zeros((8 - planes - 2, length), F32)
    for i, (df, ds) in enumerate(DIRS):
        @pl.when(valid(df, ds))
        def _(i=i, df=df, ds=ds):
            part_copy(i, df, ds).start()

    for df in (-1, 1):
        @pl.when(valid(-df, 0))
        def _(df=df):
            hw_copy(df).wait_recv()

    def make_taps(p, carry):
        h = hwb[p]
        h2 = h * h

        def profile(d, reach, reach2):
            d = d.astype(F32)
            return jnp.where(jnp.abs(d) <= reach, jnp.exp(-2.0 * (d * d) / reach2), 0.0)

        lane = iota((8, 256), 1)
        small = jnp.where(lane <= 2 * MAXH, profile(lane - MAXH, h, h2), 0.0)
        inv = 1.0 / jnp.sqrt(jnp.sum(small * small, axis=1, keepdims=True))
        inv = jnp.broadcast_to(inv, (8, 256))[0:1]
        h, h2 = h[0:1], h2[0:1]
        shape = (3 * BLOCK, BLOCK)
        val = profile(iota(shape, 0) - BLOCK - iota(shape, 1), h[:, :BLOCK], h2[:, :BLOCK]) * inv[:, :BLOCK]
        hi = val.astype(BF16)
        tcol[p, :, 0:BLOCK] = hi
        tcol[p, :, BLOCK:] = (val - hi.astype(F32)).astype(BF16)
        shape = (BROWS, 256)
        lane = iota(shape, 1)
        row = row_of(iota(shape, 0), rows)
        val = profile(lax.rem(lane, tall) - HALO - row, h, h2) * inv
        hi = val.astype(BF16).astype(F32)
        trow[p] = jnp.where(lane < 2 * tall, hi, val - hi).astype(BF16)
        return carry

    lax.fori_loop(0, planes + 2, make_taps, 0)

    def blur(src, p, t, height):
        blocks = length // BLOCK
        field = jnp.concatenate(
            [src[p, :, j * BLOCK:(j + 3) * BLOCK] for j in range(blocks)], axis=0)
        both = jnp.dot(field, tcol[t], preferred_element_type=F32)
        q = both[:, :BLOCK] + both[:, BLOCK:]
        hi = q.astype(BF16)
        lo = (q - hi.astype(F32)).astype(BF16)
        hi = jnp.concatenate([hi[j * tall:(j + 1) * tall] for j in range(blocks)], axis=1)
        lo = jnp.concatenate([lo[j * tall:(j + 1) * tall] for j in range(blocks)], axis=1)
        return jnp.dot(trow[t][:height, :3 * tall], jnp.concatenate([hi, lo, hi], axis=0),
                       preferred_element_type=F32)

    own.wait()
    for i, (df, ds) in enumerate(DIRS):
        @pl.when(valid(-df, -ds))
        def _(i=i, df=df, ds=ds):
            sky_copy(i, df, ds).wait_recv()

    def make_beam(p, carry):
        beam = blur(skyh, p, p, BROWS)
        r = iota(beam.shape, 0)
        outside = jnp.logical_or(jnp.logical_and(r == rows, si == ns - 1),
                                 jnp.logical_and(r == rows + 1, si == 0))
        beam = jnp.where(outside, 0.0, beam)
        bs[p, 0] = shift_prev(beam).astype(BF16)
        bs[p, 1] = beam.astype(BF16)
        bs[p, 2] = shift_next(beam).astype(BF16)
        return carry

    lax.fori_loop(0, planes + 2, make_beam, 0)

    for i, (df, ds) in enumerate(DIRS):
        @pl.when(valid(-df, -ds))
        def _(i=i, df=df, ds=ds):
            part_copy(i, df, ds).wait_recv()
    r = iota((rows, length), 0)
    for f in range(planes):
        total = part[f + 1, 0:rows]
        if f == 0:
            total = total + pf[0]
        if f == planes - 1:
            total = total + pf[1]
        for up in (0, 1):
            line = pe[2 + up, f + 1:f + 2]
            if f == 0:
                line = line + pe[4 + up, planes + 1:planes + 2]
            if f == planes - 1:
                line = line + pe[up, 0:1]
            total = total + jnp.where(r == (0 if up else rows - 1), line, 0.0)
        gbh[f, HALO:HALO + rows, PAD:PAD + length] = total.astype(BF16)
    for ds in (-1, 1):
        @pl.when(valid(0, ds))
        def _(ds=ds):
            gb_copy(ds).start()

    def gram(g, total):
        left = bs[pl.ds(g, 3)].reshape(9 * BROWS, length)
        return total + lax.dot_general(left, cotv[g].reshape(wide, length),
                                       (((1,), (1,)), ((), ())), preferred_element_type=F32)

    acc2 = lax.fori_loop(0, planes, gram, jnp.zeros((9 * BROWS, wide), F32))
    masks = [band_mask(b, BROWS, rows, wide) for b in range(3)]
    lines = []
    for a in range(3):
        for b in range(3):
            for e in range(3):
                tile = acc2[(3 * a + e) * BROWS:(3 * a + e + 1) * BROWS]
                lines.append(jnp.sum(jnp.where(masks[b], tile, 0.0), axis=0, keepdims=True))
    lines.append(jnp.zeros((128 - 27, wide), F32))
    terms = lax.dot_general(member.astype(F32), jnp.concatenate(lines, axis=0),
                            (((1,), (1,)), ((), ())), precision=lax.Precision.HIGHEST,
                            preferred_element_type=F32)
    mine[...] = terms
    slots[si] = terms

    def kg_copy(k, src, dst, send, recv, at, size, axis):
        to = lax.rem(at + k, size)
        return pltpu.make_async_remote_copy(
            src_ref=src, dst_ref=dst.at[at], send_sem=send.at[k], recv_sem=recv.at[k],
            device_id=(to, si) if axis == 0 else (fi, to), device_id_type=MESH)

    def kg_wait(k, src, dst, send, recv, at, size, axis):
        pltpu.make_async_remote_copy(
            src_ref=src, dst_ref=dst.at[lax.rem(at - k + size, size)], send_sem=send.at[k],
            recv_sem=recv.at[k], device_id=(fi, si), device_id_type=MESH).wait_recv()

    over_sky = (mine, slots, s_kg, r_kg, si, ns, 1)
    over_freq = (mine2, slots2, s_kf, r_kf, fi, nf, 0)
    for k in range(1, ns):
        kg_copy(k, *over_sky).start()

    for ds in (-1, 1):
        @pl.when(valid(0, -ds))
        def _(ds=ds):
            gb_copy(ds).wait_recv()

    def finish(f, carry):
        out_ref[f] = blur(gbh, f, f + 1, rows)
        return carry

    lax.fori_loop(0, planes // 2, finish, 0)
    for k in range(1, ns):
        kg_wait(k, *over_sky)
    total = slots[0]
    for k in range(1, ns):
        total = total + slots[k]
    mine2[...] = total
    slots2[fi] = total
    for k in range(1, nf):
        kg_copy(k, *over_freq).start()
    lax.fori_loop(planes // 2, planes, finish, 0)
    for k in range(1, nf):
        kg_wait(k, *over_freq)
    total = slots2[0]
    for k in range(1, nf):
        total = total + slots2[k]
    kg_ref[...] = total[:, :27] * scale

    for i, (df, ds) in enumerate(DIRS):
        @pl.when(valid(df, ds))
        def _(i=i, df=df, ds=ds):
            sky_copy(i, df, ds).wait_send()
            part_copy(i, df, ds).wait_send()
            if ds == 0:
                hw_copy(df).wait_send()
            if df == 0:
                gb_copy(ds).wait_send()
    for k in range(1, ns):
        kg_copy(k, *over_sky).wait_send()
    for k in range(1, nf):
        kg_copy(k, *over_freq).wait_send()


def per_device(sky_cube, half_width, conv_weight, out_cotangent):
    planes, rows, length = sky_cube.shape
    chans = conv_weight.shape[0]
    nf, ns = lax.axis_size("freq"), lax.axis_size("sky")
    scale = 1.0 / math.sqrt(planes * nf * rows * ns * length)
    tall = rows + 2 * HALO
    wide = chans * rows
    dma = pltpu.SemaphoreType.DMA

    def kernel(*refs):
        body(nf, ns, scale, *refs)

    return pl.pallas_call(
        kernel,
        out_shape=(jax.ShapeDtypeStruct((planes, rows, length), F32),
                   jax.ShapeDtypeStruct((chans, 27), F32)),
        in_specs=[pl.BlockSpec(memory_space=pltpu.SMEM), pl.BlockSpec(memory_space=pl.ANY),
                  pl.BlockSpec(memory_space=pltpu.VMEM), pl.BlockSpec(memory_space=pl.ANY)],
        out_specs=(pl.BlockSpec(memory_space=pltpu.VMEM), pl.BlockSpec(memory_space=pltpu.VMEM)),
        scratch_shapes=[
            pltpu.VMEM((planes + 2, tall, length + 2 * PAD), BF16),
            pltpu.VMEM((planes, tall, length + 2 * PAD), BF16),
            pltpu.VMEM((planes, chans, rows, length), BF16),
            pltpu.VMEM((9 * EDGE, wide), F32),
            pltpu.VMEM((planes + 2, 3, EDGE, length), F32),
            pltpu.VMEM((planes + 2, EDGE, length), F32),
            pltpu.VMEM((8, length), F32),
            pltpu.VMEM((8, length), F32),
            pltpu.VMEM((2, rows, length), F32),
            pltpu.VMEM((6, 8, length), F32),
            pltpu.VMEM((planes + 2, 3, BROWS, length), BF16),
            pltpu.VMEM((planes + 2, 3 * BLOCK, 2 * BLOCK), BF16),
            pltpu.VMEM((planes + 2, BROWS, 256), BF16),
            pltpu.VMEM((planes + 2, 8, 256), F32),
            pltpu.VMEM((chans, 128), F32),
            pltpu.VMEM((ns, chans, 128), F32),
            pltpu.VMEM((chans, 128), F32),
            pltpu.VMEM((nf, chans, 128), F32),
            dma((planes,)), dma((1,)),
            dma((8,)), dma((8,)), dma((2,)), dma((2,)), dma((8,)), dma((8,)), dma((2,)), dma((2,)),
            dma((ns,)), dma((ns,)), dma((nf,)), dma((nf,)),
        ],
        compiler_params=pltpu.CompilerParams(
            collective_id=0, has_side_effects=True, vmem_limit_bytes=48 * 1024 * 1024),
        name="beam_backward",
    )(half_width, sky_cube, conv_weight, out_cotangent)


def solution(mesh):
    return jax.shard_map(
        per_device,
        mesh=mesh,
        in_specs=(P("freq", "sky", None), P("freq"), P(), P(None, "freq", "sky", None)),
        out_specs=(P("freq", "sky", None), P()),
        check_vma=False,
    )
```

```python
import math

import jax
import jax.numpy as jnp
from jax import lax
from jax.experimental import pallas as pl
from jax.experimental.pallas import tpu as pltpu
from jax.sharding import PartitionSpec as P

MAXH = 12
HALO = 16
PAD = 128
BLOCK = 128
EDGE = 40
BROWS = 48
TALL3 = 128
F32 = jnp.float32
BF16 = jnp.bfloat16
MESH = pl.DeviceIdType.MESH
DIRS = [(df, ds) for df in (-1, 0, 1) for ds in (-1, 0, 1) if (df, ds) != (0, 0)]


def iota(shape, dim):
    return lax.broadcasted_iota(jnp.int32, shape, dim)


def row_of(r, rows):
    return jnp.where(r <= rows, r, jnp.where(r == rows + 1, -1, -1000))


def band_mask(b, height, rows, width):
    shape = (height, width)
    return row_of(iota(shape, 0), rows) == lax.rem(iota(shape, 1), rows) + (b - 1)


def shift_next(x):
    n = x.shape[-1]
    return jnp.where(iota(x.shape, 1) == n - 1, 0.0, pltpu.roll(x, n - 1, 1))


def shift_prev(x):
    n = x.shape[-1]
    return jnp.where(iota(x.shape, 1) == 0, 0.0, pltpu.roll(x, 1, 1))


def body(nf, ns, scale, hw_hbm, sky_ref, w_hbm, cot_ref, out_ref, kg_ref,
         outv, out_sem, hw_ref, w_ref, skyh, gbh, cotv, bmat, acc, part, eu, ed, pf, pe, bs, tcol, trow, hwb,
         mine, slots, mine2, slots2,
         cot_sem, own_sem, s_sky, r_sky, s_hw, r_hw, s_part, r_part, s_gb, r_gb,
         s_kg, r_kg, s_kf, r_kf):
    planes, rows, length = out_ref.shape
    chans = w_ref.shape[0]
    wide = chans * rows
    tall = rows + 2 * HALO
    fi, si = lax.axis_index("freq"), lax.axis_index("sky")

    def valid(df, ds):
        ok = None
        for at, step, size in ((fi, df, nf), (si, ds, ns)):
            if step:
                one = at + step < size if step > 0 else at + step >= 0
                ok = one if ok is None else jnp.logical_and(ok, one)
        return ok

    def span(step, own_lo, own_n, halo_n, full_n):
        if step == 0:
            return own_lo, 0, own_n
        if step > 0:
            return own_lo - halo_n, own_n - halo_n, halo_n
        return own_lo + own_n, 0, halo_n

    lanes = pl.ds(PAD, length)

    own_w = pltpu.make_async_copy(w_hbm, w_ref, own_sem.at[1])
    own_w.start()
    own_hw = pltpu.make_async_copy(hw_hbm, hw_ref, own_sem.at[2])
    own_hw.start()
    cot_copies = [pltpu.make_async_copy(cot_ref.at[:, g], cotv.at[g], cot_sem.at[g])
                  for g in range(planes)]
    for copy in cot_copies:
        copy.start()
    own = pltpu.make_async_copy(
        sky_ref, skyh.at[pl.ds(1, planes), pl.ds(HALO, rows), lanes], own_sem.at[0])
    own.start()

    def dst_sky(df, ds):
        p0, _, pn = span(df, 1, planes, 1, planes + 2)
        r0, _, rn = span(ds, HALO, rows, HALO, tall)
        return skyh.at[pl.ds(p0, pn), pl.ds(r0, rn), lanes]

    for i, (df, ds) in enumerate(DIRS):
        @pl.when(jnp.logical_not(valid(-df, -ds)))
        def _(df=df, ds=ds):
            ref = dst_sky(df, ds)
            ref[...] = jnp.zeros(ref.shape, BF16)
            if df == 0:
                r0, _, rn = span(ds, HALO, rows, HALO, tall)
                gbh[:, r0:r0 + rn, PAD:PAD + length] = jnp.zeros((planes, rn, length), BF16)
            if ds == 0:
                hwb[0 if df > 0 else planes + 1] = jnp.ones((8, 256), F32)
                pf[0 if df > 0 else 1] = jnp.zeros((rows, length), F32)
            else:
                pe[(df + 1) * 2 + (ds > 0)] = jnp.zeros((8, length), F32)

    barrier = pltpu.get_barrier_semaphore()
    for k in range(1, ns):
        pl.semaphore_signal(barrier, inc=1, device_id=(fi, lax.rem(si + k, ns)), device_id_type=MESH)
    for k in range(1, nf):
        pl.semaphore_signal(barrier, inc=1, device_id=(lax.rem(fi + k, nf), si), device_id_type=MESH)
    greeted = jnp.int32(ns + nf - 2)
    for df, ds in DIRS:
        if df and ds:
            ok = valid(df, ds)
            greeted = greeted + jnp.where(ok, 1, 0)

            @pl.when(ok)
            def _(df=df, ds=ds):
                pl.semaphore_signal(barrier, inc=1, device_id=(fi + df, si + ds), device_id_type=MESH)

    for ref in (skyh, gbh):
        n = ref.shape[0]
        ref[:, :, 0:PAD] = jnp.zeros((n, tall, PAD), BF16)
        ref[:, :, PAD + length:] = jnp.zeros((n, tall, PAD), BF16)
    own_hw.wait()
    for k in range(planes):
        hwb[1 + k] = jnp.full((8, 256), hw_ref[k].astype(F32))
    own_w.wait()
    member = (lax.div(iota((chans, wide), 1), rows) == iota((chans, wide), 0))
    spread = lax.dot_general(w_ref[...], member.astype(BF16), (((0,), (0,)), ((), ())),
                             preferred_element_type=F32)
    masks = [band_mask(b, EDGE, rows, wide) for b in range(3)]
    tiles = []
    for a in range(3):
        for e in range(3):
            tile = jnp.zeros((EDGE, wide), F32)
            for b in range(3):
                k = 9 * a + 3 * b + e
                tile = tile + jnp.where(masks[b], spread[k:k + 1, :], 0.0)
            tiles.append(tile)
    tiles.append(jnp.zeros((8, wide), F32))
    bmat[...] = jnp.concatenate(tiles, axis=0).astype(BF16)

    pl.semaphore_wait(barrier, greeted)

    def remote(src, dst, send, recv, df, ds):
        return pltpu.make_async_remote_copy(
            src_ref=src, dst_ref=dst, send_sem=send, recv_sem=recv,
            device_id=(fi + df, si + ds), device_id_type=MESH)

    def sky_copy(i, df, ds):
        _, p0, pn = span(df, 1, planes, 1, planes + 2)
        _, r0, rn = span(ds, HALO, rows, HALO, tall)
        return remote(sky_ref.at[pl.ds(p0, pn), pl.ds(r0, rn), :], dst_sky(df, ds),
                      s_sky.at[i], r_sky.at[i], df, ds)

    def hw_copy(df):
        j = 0 if df > 0 else 1
        return remote(hwb.at[planes if df > 0 else 1], hwb.at[0 if df > 0 else planes + 1],
                      s_hw.at[j], r_hw.at[j], df, 0)

    def part_copy(i, df, ds):
        if ds == 0:
            src, dst = part.at[planes + 1 if df > 0 else 0, pl.ds(0, rows)], pf.at[0 if df > 0 else 1]
        else:
            src, dst = (ed if ds > 0 else eu), pe.at[(df + 1) * 2 + (ds > 0)]
        return remote(src, dst, s_part.at[i], r_part.at[i], df, ds)

    def gb_copy(ds):
        j = 0 if ds > 0 else 1
        r0, r1, rn = span(ds, HALO, rows, HALO, tall)
        return remote(gbh.at[:, pl.ds(HALO + r1, rn), :], gbh.at[:, pl.ds(r0, rn), :],
                      s_gb.at[j], r_gb.at[j], 0, ds)

    for i, (df, ds) in enumerate(DIRS):
        @pl.when(valid(df, ds))
        def _(i=i, df=df, ds=ds):
            sky_copy(i, df, ds).start()
            if ds == 0:
                hw_copy(df).start()

    def close_plane(p):
        total = acc[p, 1] + shift_next(acc[p, 0]) + shift_prev(acc[p, 2])
        part[p] = total
        ed[p:p + 1, :] = total[rows:rows + 1]
        eu[p:p + 1, :] = total[rows + 1:rows + 2]

    for g in range(planes):
        cot_copies[g].wait()
        res = jnp.dot(bmat[...], cotv[g].reshape(wide, length), preferred_element_type=F32)
        for a in range(3):
            piece = res[3 * a * EDGE:3 * (a + 1) * EDGE].reshape(3, EDGE, length)
            if g == 0 or a == 2:
                acc[g + a] = piece
            else:
                acc[g + a] += piece
        close_plane(g)
    close_plane(planes)
    close_plane(planes + 1)
    eu[planes + 2:, :] = jnp.zeros((8 - planes - 2, length), F32)
    ed[planes + 2:, :] = jnp.zeros((8 - planes - 2, length), F32)
    for i, (df, ds) in enumerate(DIRS):
        @pl.when(valid(df, ds))
        def _(i=i, df=df, ds=ds):
            part_copy(i, df, ds).start()

    for df in (-1, 1):
        @pl.when(valid(-df, 0))
        def _(df=df):
            hw_copy(df).wait_recv()

    def make_taps(p):
        h = hwb[p]
        h2 = h * h

        def profile(d, reach, reach2):
            d = d.astype(F32)
            return jnp.where(jnp.abs(d) <= reach, jnp.exp(-2.0 * (d * d) / reach2), 0.0)

        lane = iota((8, 256), 1)
        small = jnp.where(lane <= 2 * MAXH, profile(lane - MAXH, h, h2), 0.0)
        inv = 1.0 / jnp.sqrt(jnp.sum(small * small, axis=1, keepdims=True))
        inv = jnp.broadcast_to(inv, (8, 256))[0:1]
        h, h2 = h[0:1], h2[0:1]
        shape = (3 * BLOCK, BLOCK)
        val = profile(iota(shape, 0) - BLOCK - iota(shape, 1), h[:, :BLOCK], h2[:, :BLOCK]) * inv[:, :BLOCK]
        hi = val.astype(BF16)
        tcol[p, :, 0:BLOCK] = hi
        tcol[p, :, BLOCK:] = (val - hi.astype(F32)).astype(BF16)
        shape = (BROWS, 256)
        lane = iota(shape, 1)
        row = row_of(iota(shape, 0), rows)
        val = profile(lax.rem(lane, tall) - HALO - row, h, h2) * inv
        hi = val.astype(BF16).astype(F32)
        trow[p] = jnp.where(lane < 2 * tall, hi, val - hi).astype(BF16)

    for p in range(planes + 2):
        make_taps(p)

    def blur(src, p, t, height):
        blocks = length // BLOCK
        field = jnp.concatenate(
            [src[p, :, j * BLOCK:(j + 3) * BLOCK] for j in range(blocks)], axis=0)
        both = jnp.dot(field, tcol[t], preferred_element_type=F32)
        q = both[:, :BLOCK] + both[:, BLOCK:]
        hi = q.astype(BF16)
        lo = (q - hi.astype(F32)).astype(BF16)
        hi = jnp.concatenate([hi[j * tall:(j + 1) * tall] for j in range(blocks)], axis=1)
        lo = jnp.concatenate([lo[j * tall:(j + 1) * tall] for j in range(blocks)], axis=1)
        return jnp.dot(trow[t][:height, :3 * tall], jnp.concatenate([hi, lo, hi], axis=0),
                       preferred_element_type=F32)

    own.wait()
    for i, (df, ds) in enumerate(DIRS):
        @pl.when(valid(-df, -ds))
        def _(i=i, df=df, ds=ds):
            sky_copy(i, df, ds).wait_recv()

    for p in range(planes + 2):
        beam = blur(skyh, p, p, BROWS)[:EDGE]
        r = iota(beam.shape, 0)
        outside = jnp.logical_or(jnp.logical_and(r == rows, si == ns - 1),
                                 jnp.logical_and(r == rows + 1, si == 0))
        beam = jnp.where(outside, 0.0, beam)
        bs[p] = jnp.concatenate(
            [shift_prev(beam), beam, shift_next(beam), jnp.zeros((8, length), F32)],
            axis=0).astype(BF16)

    for i, (df, ds) in enumerate(DIRS):
        @pl.when(valid(-df, -ds))
        def _(i=i, df=df, ds=ds):
            part_copy(i, df, ds).wait_recv()
    r = iota((rows, length), 0)
    for f in range(planes):
        total = part[f + 1, 0:rows]
        if f == 0:
            total = total + pf[0]
        if f == planes - 1:
            total = total + pf[1]
        for up in (0, 1):
            line = pe[2 + up, f + 1:f + 2]
            if f == 0:
                line = line + pe[4 + up, planes + 1:planes + 2]
            if f == planes - 1:
                line = line + pe[up, 0:1]
            total = total + jnp.where(r == (0 if up else rows - 1), line, 0.0)
        gbh[f, HALO:HALO + rows, PAD:PAD + length] = total.astype(BF16)
    for ds in (-1, 1):
        @pl.when(valid(0, ds))
        def _(ds=ds):
            gb_copy(ds).start()

    acc2 = jnp.zeros((3 * TALL3, wide), F32)
    for g in range(planes):
        acc2 = acc2 + lax.dot_general(
            bs[g:g + 3].reshape(3 * TALL3, length), cotv[g].reshape(wide, length),
            (((1,), (1,)), ((), ())), preferred_element_type=F32)
    lines = []
    for a in range(3):
        for b in range(3):
            for e in range(3):
                tile = acc2[a * TALL3 + e * EDGE:a * TALL3 + (e + 1) * EDGE]
                lines.append(jnp.sum(jnp.where(masks[b], tile, 0.0), axis=0, keepdims=True))
    lines.append(jnp.zeros((128 - 27, wide), F32))
    terms = lax.dot_general(member.astype(F32), jnp.concatenate(lines, axis=0),
                            (((1,), (1,)), ((), ())), precision=lax.Precision.HIGHEST,
                            preferred_element_type=F32)
    half = chans // 2
    packed = terms[:half] + pltpu.roll(terms[half:], 64, 1)
    mine[...] = packed
    slots[si] = packed

    def kg_copy(k, src, dst, send, recv, at, size, axis):
        to = lax.rem(at + k, size)
        return pltpu.make_async_remote_copy(
            src_ref=src, dst_ref=dst.at[at], send_sem=send.at[k], recv_sem=recv.at[k],
            device_id=(to, si) if axis == 0 else (fi, to), device_id_type=MESH)

    def kg_wait(k, src, dst, send, recv, at, size, axis):
        pltpu.make_async_remote_copy(
            src_ref=src, dst_ref=dst.at[lax.rem(at - k + size, size)], send_sem=send.at[k],
            recv_sem=recv.at[k], device_id=(fi, si), device_id_type=MESH).wait_recv()

    over_sky = (mine, slots, s_kg, r_kg, si, ns, 1)
    over_freq = (mine2, slots2, s_kf, r_kf, fi, nf, 0)
    for k in range(1, ns):
        kg_copy(k, *over_sky).start()

    for ds in (-1, 1):
        @pl.when(valid(0, -ds))
        def _(ds=ds):
            gb_copy(ds).wait_recv()

    out_copies = [pltpu.make_async_copy(outv.at[f], out_ref.at[f], out_sem.at[f])
                  for f in range(planes)]

    def finish(f):
        outv[f] = blur(gbh, f, f + 1, rows)
        out_copies[f].start()

    for f in range(planes // 2):
        finish(f)
    for k in range(1, ns):
        kg_wait(k, *over_sky)
    total = slots[0]
    for k in range(1, ns):
        total = total + slots[k]
    mine2[...] = total
    slots2[fi] = total
    for k in range(1, nf):
        kg_copy(k, *over_freq).start()
    for f in range(planes // 2, planes):
        finish(f)
    for k in range(1, nf):
        kg_wait(k, *over_freq)
    total = slots2[0]
    for k in range(1, nf):
        total = total + slots2[k]
    total = total * scale
    kg_ref[0:half] = total[:, :27]
    kg_ref[half:] = pltpu.roll(total, 64, 1)[:, :27]

    for copy in out_copies:
        copy.wait()
    for i, (df, ds) in enumerate(DIRS):
        @pl.when(valid(df, ds))
        def _(i=i, df=df, ds=ds):
            sky_copy(i, df, ds).wait_send()
            part_copy(i, df, ds).wait_send()
            if ds == 0:
                hw_copy(df).wait_send()
            if df == 0:
                gb_copy(ds).wait_send()
    for k in range(1, ns):
        kg_copy(k, *over_sky).wait_send()
    for k in range(1, nf):
        kg_copy(k, *over_freq).wait_send()


def per_device(sky_cube, half_width, conv_weight, out_cotangent):
    planes, rows, length = sky_cube.shape
    chans = conv_weight.shape[0]
    nf, ns = lax.axis_size("freq"), lax.axis_size("sky")
    scale = 1.0 / math.sqrt(planes * nf * rows * ns * length)
    tall = rows + 2 * HALO
    wide = chans * rows
    dma = pltpu.SemaphoreType.DMA

    def kernel(*refs):
        body(nf, ns, scale, *refs)

    return pl.pallas_call(
        kernel,
        out_shape=(jax.ShapeDtypeStruct((planes, rows, length), F32),
                   jax.ShapeDtypeStruct((chans, 27), F32)),
        in_specs=[pl.BlockSpec(memory_space=pltpu.HBM)] * 4,
        out_specs=(pl.BlockSpec(memory_space=pltpu.HBM), pl.BlockSpec(memory_space=pltpu.VMEM)),
        scratch_shapes=[
            pltpu.VMEM((planes, rows, length), F32), dma((planes,)),
            pltpu.SMEM((planes,), jnp.int32),
            pltpu.VMEM((chans, 27), BF16),
            pltpu.VMEM((planes + 2, tall, length + 2 * PAD), BF16),
            pltpu.VMEM((planes, tall, length + 2 * PAD), BF16),
            pltpu.VMEM((planes, chans, rows, length), BF16),
            pltpu.VMEM((9 * EDGE + 8, wide), BF16),
            pltpu.VMEM((planes + 2, 3, EDGE, length), F32),
            pltpu.VMEM((planes + 2, EDGE, length), F32),
            pltpu.VMEM((8, length), F32),
            pltpu.VMEM((8, length), F32),
            pltpu.VMEM((2, rows, length), F32),
            pltpu.VMEM((6, 8, length), F32),
            pltpu.VMEM((planes + 2, TALL3, length), BF16),
            pltpu.VMEM((planes + 2, 3 * BLOCK, 2 * BLOCK), BF16),
            pltpu.VMEM((planes + 2, BROWS, 256), BF16),
            pltpu.VMEM((planes + 2, 8, 256), F32),
            pltpu.VMEM((chans // 2, 128), F32),
            pltpu.VMEM((ns, chans // 2, 128), F32),
            pltpu.VMEM((chans // 2, 128), F32),
            pltpu.VMEM((nf, chans // 2, 128), F32),
            dma((planes,)), dma((3,)),
            dma((8,)), dma((8,)), dma((2,)), dma((2,)), dma((8,)), dma((8,)), dma((2,)), dma((2,)),
            dma((ns,)), dma((ns,)), dma((nf,)), dma((nf,)),
        ],
        compiler_params=pltpu.CompilerParams(
            collective_id=0, has_side_effects=True, vmem_limit_bytes=60 * 1024 * 1024),
        name="beam_backward",
    )(half_width, sky_cube, conv_weight, out_cotangent)


def solution(mesh):
    return jax.shard_map(
        per_device,
        mesh=mesh,
        in_specs=(P("freq", "sky", None), P("freq"), P(), P(None, "freq", "sky", None)),
        out_specs=(P("freq", "sky", None), P()),
        check_vma=False,
    )
```

```python
import math

import jax
import jax.numpy as jnp
from jax import lax
from jax.experimental import pallas as pl
from jax.experimental.pallas import tpu as pltpu
from jax.sharding import PartitionSpec as P

MAXH = 12
HALO = 16
PAD = 128
BLOCK = 128
HALF = 16
EDGE = 24
TALL3 = 80
F32 = jnp.float32
BF16 = jnp.bfloat16
MESH = pl.DeviceIdType.MESH
DIRS = [(df, ds) for df in (-1, 0, 1) for ds in (-1, 0, 1) if (df, ds) != (0, 0)]


def iota(shape, dim):
    return lax.broadcasted_iota(jnp.int32, shape, dim)


def row_of(r, rows):
    return jnp.where(r <= rows, r, jnp.where(r == rows + 1, -1, -1000))


def band_mask(b, height, rows, width):
    shape = (height, width)
    return row_of(iota(shape, 0), rows) == lax.rem(iota(shape, 1), rows) + (b - 1)


def shift_next(x):
    n = x.shape[-1]
    return jnp.where(iota(x.shape, 1) == n - 1, 0.0, pltpu.roll(x, n - 1, 1))


def shift_prev(x):
    n = x.shape[-1]
    return jnp.where(iota(x.shape, 1) == 0, 0.0, pltpu.roll(x, 1, 1))


def body(nf, ns, scale, hw_hbm, sky_ref, w_hbm, cot_ref, out_ref, kg_ref,
         outv, out_sem, hw_ref, w_ref, skyh, gbh, cotv, bmat, acc, part, eu, ed, pf, pe, bs, tcol, trow, hwb,
         mine, slots, mine2, slots2,
         cot_sem, own_sem, s_sky, r_sky, s_hw, r_hw, s_part, r_part, s_gb, r_gb,
         s_kg, r_kg, s_kf, r_kf):
    planes, rows, length = out_ref.shape
    chans = w_ref.shape[0]
    wide = chans * HALF
    halves = rows // HALF
    high = halves * EDGE
    tall = rows + 2 * HALO
    fi, si = lax.axis_index("freq"), lax.axis_index("sky")

    def valid(df, ds):
        ok = None
        for at, step, size in ((fi, df, nf), (si, ds, ns)):
            if step:
                one = at + step < size if step > 0 else at + step >= 0
                ok = one if ok is None else jnp.logical_and(ok, one)
        return ok

    def span(step, own_lo, own_n, halo_n, full_n):
        if step == 0:
            return own_lo, 0, own_n
        if step > 0:
            return own_lo - halo_n, own_n - halo_n, halo_n
        return own_lo + own_n, 0, halo_n

    lanes = pl.ds(PAD, length)

    own_w = pltpu.make_async_copy(w_hbm, w_ref, own_sem.at[1])
    own_w.start()
    own_hw = pltpu.make_async_copy(hw_hbm, hw_ref, own_sem.at[2])
    own_hw.start()
    cot_copies = [pltpu.make_async_copy(cot_ref.at[:, g], cotv.at[g], cot_sem.at[g])
                  for g in range(planes)]
    for copy in cot_copies:
        copy.start()
    own = pltpu.make_async_copy(
        sky_ref, skyh.at[pl.ds(1, planes), pl.ds(HALO, rows), lanes], own_sem.at[0])
    own.start()

    def dst_sky(df, ds):
        p0, _, pn = span(df, 1, planes, 1, planes + 2)
        r0, _, rn = span(ds, HALO, rows, HALO, tall)
        return skyh.at[pl.ds(p0, pn), pl.ds(r0, rn), lanes]

    for i, (df, ds) in enumerate(DIRS):
        @pl.when(jnp.logical_not(valid(-df, -ds)))
        def _(df=df, ds=ds):
            ref = dst_sky(df, ds)
            ref[...] = jnp.zeros(ref.shape, BF16)
            if df == 0:
                r0, _, rn = span(ds, HALO, rows, HALO, tall)
                gbh[:, r0:r0 + rn, PAD:PAD + length] = jnp.zeros((planes, rn, length), BF16)
            if ds == 0:
                hwb[0 if df > 0 else planes + 1] = jnp.ones((8, 256), F32)
                pf[0 if df > 0 else 1] = jnp.zeros((rows, length), F32)
            else:
                pe[(df + 1) * 2 + (ds > 0)] = jnp.zeros((8, length), F32)

    barrier = pltpu.get_barrier_semaphore()
    for k in range(1, ns):
        pl.semaphore_signal(barrier, inc=1, device_id=(fi, lax.rem(si + k, ns)), device_id_type=MESH)
    for k in range(1, nf):
        pl.semaphore_signal(barrier, inc=1, device_id=(lax.rem(fi + k, nf), si), device_id_type=MESH)
    greeted = jnp.int32(ns + nf - 2)
    for df, ds in DIRS:
        if df and ds:
            ok = valid(df, ds)
            greeted = greeted + jnp.where(ok, 1, 0)

            @pl.when(ok)
            def _(df=df, ds=ds):
                pl.semaphore_signal(barrier, inc=1, device_id=(fi + df, si + ds), device_id_type=MESH)

    for ref in (skyh, gbh):
        n = ref.shape[0]
        ref[:, :, 0:PAD] = jnp.zeros((n, tall, PAD), BF16)
        ref[:, :, PAD + length:] = jnp.zeros((n, tall, PAD), BF16)
    own_hw.wait()
    for k in range(planes):
        hwb[1 + k] = jnp.full((8, 256), hw_ref[k].astype(F32))
    own_w.wait()
    member = (lax.div(iota((chans, wide), 1), HALF) == iota((chans, wide), 0))
    spread = lax.dot_general(w_ref[...], member.astype(BF16), (((0,), (0,)), ((), ())),
                             preferred_element_type=F32)
    masks = [band_mask(b, EDGE, HALF, wide) for b in range(3)]
    tiles = []
    for a in range(3):
        for e in range(3):
            tile = jnp.zeros((EDGE, wide), F32)
            for b in range(3):
                k = 9 * a + 3 * b + e
                tile = tile + jnp.where(masks[b], spread[k:k + 1, :], 0.0)
            tiles.append(tile)
    tiles.append(jnp.zeros((8, wide), F32))
    bmat[...] = jnp.concatenate(tiles, axis=0).astype(BF16)

    pl.semaphore_wait(barrier, greeted)

    def remote(src, dst, send, recv, df, ds):
        return pltpu.make_async_remote_copy(
            src_ref=src, dst_ref=dst, send_sem=send, recv_sem=recv,
            device_id=(fi + df, si + ds), device_id_type=MESH)

    def sky_copy(i, df, ds):
        _, p0, pn = span(df, 1, planes, 1, planes + 2)
        _, r0, rn = span(ds, HALO, rows, HALO, tall)
        return remote(sky_ref.at[pl.ds(p0, pn), pl.ds(r0, rn), :], dst_sky(df, ds),
                      s_sky.at[i], r_sky.at[i], df, ds)

    def hw_copy(df):
        j = 0 if df > 0 else 1
        return remote(hwb.at[planes if df > 0 else 1], hwb.at[0 if df > 0 else planes + 1],
                      s_hw.at[j], r_hw.at[j], df, 0)

    def part_copy(i, df, ds):
        if ds == 0:
            src, dst = part.at[planes + 1 if df > 0 else 0, pl.ds(0, rows)], pf.at[0 if df > 0 else 1]
        else:
            src, dst = (ed if ds > 0 else eu), pe.at[(df + 1) * 2 + (ds > 0)]
        return remote(src, dst, s_part.at[i], r_part.at[i], df, ds)

    def gb_copy(ds):
        j = 0 if ds > 0 else 1
        r0, r1, rn = span(ds, HALO, rows, HALO, tall)
        return remote(gbh.at[:, pl.ds(HALO + r1, rn), :], gbh.at[:, pl.ds(r0, rn), :],
                      s_gb.at[j], r_gb.at[j], 0, ds)

    for i, (df, ds) in enumerate(DIRS):
        @pl.when(valid(df, ds))
        def _(i=i, df=df, ds=ds):
            sky_copy(i, df, ds).start()
            if ds == 0:
                hw_copy(df).start()

    def cot_half(g, h):
        return cotv[g, :, h * HALF:(h + 1) * HALF, :].reshape(wide, length)

    def close_plane(p):
        r = iota((HALF, length), 0)
        piece = [acc[p, h, 1] + shift_next(acc[p, h, 0]) + shift_prev(acc[p, h, 2])
                 for h in range(halves)]
        for h in range(halves):
            total = piece[h][:HALF]
            if h > 0:
                total = total + jnp.where(r == 0, piece[h - 1][HALF:HALF + 1], 0.0)
            if h < halves - 1:
                total = total + jnp.where(r == HALF - 1, piece[h + 1][HALF + 1:HALF + 2], 0.0)
            part[p, h * HALF:(h + 1) * HALF] = total
        ed[p:p + 1, :] = piece[-1][HALF:HALF + 1]
        eu[p:p + 1, :] = piece[0][HALF + 1:HALF + 2]

    for g in range(planes):
        cot_copies[g].wait()
        for h in range(halves):
            res = jnp.dot(bmat[...], cot_half(g, h), preferred_element_type=F32)
            for a in range(3):
                piece = res[3 * a * EDGE:3 * (a + 1) * EDGE].reshape(3, EDGE, length)
                if g == 0 or a == 2:
                    acc[g + a, h] = piece
                else:
                    acc[g + a, h] += piece
        close_plane(g)
    close_plane(planes)
    close_plane(planes + 1)
    eu[planes + 2:, :] = jnp.zeros((8 - planes - 2, length), F32)
    ed[planes + 2:, :] = jnp.zeros((8 - planes - 2, length), F32)
    for i, (df, ds) in enumerate(DIRS):
        @pl.when(valid(df, ds))
        def _(i=i, df=df, ds=ds):
            part_copy(i, df, ds).start()

    for df in (-1, 1):
        @pl.when(valid(-df, 0))
        def _(df=df):
            hw_copy(df).wait_recv()

    def make_taps(p):
        h = hwb[p]
        h2 = h * h

        def profile(d, reach, reach2):
            d = d.astype(F32)
            return jnp.where(jnp.abs(d) <= reach, jnp.exp(-2.0 * (d * d) / reach2), 0.0)

        lane = iota((8, 256), 1)
        small = jnp.where(lane <= 2 * MAXH, profile(lane - MAXH, h, h2), 0.0)
        inv = 1.0 / jnp.sqrt(jnp.sum(small * small, axis=1, keepdims=True))
        inv = jnp.broadcast_to(inv, (8, 256))[0:1]
        h, h2 = h[0:1], h2[0:1]
        shape = (3 * BLOCK, BLOCK)
        val = profile(iota(shape, 0) - BLOCK - iota(shape, 1), h[:, :BLOCK], h2[:, :BLOCK]) * inv[:, :BLOCK]
        hi = val.astype(BF16)
        tcol[p, :, 0:BLOCK] = hi
        tcol[p, :, BLOCK:] = (val - hi.astype(F32)).astype(BF16)
        shape = (high, 256)
        lane = iota(shape, 1)
        row = row_of(lax.rem(iota(shape, 0), EDGE), HALF) + HALF * lax.div(iota(shape, 0), EDGE)
        val = profile(lax.rem(lane, tall) - HALO - row, h, h2) * inv
        hi = val.astype(BF16).astype(F32)
        trow[p] = jnp.where(lane < 2 * tall, hi, val - hi).astype(BF16)

    for p in range(planes + 2):
        make_taps(p)

    def blur(src, p, t):
        blocks = length // BLOCK
        field = jnp.concatenate(
            [src[p, :, j * BLOCK:(j + 3) * BLOCK] for j in range(blocks)], axis=0)
        both = jnp.dot(field, tcol[t], preferred_element_type=F32)
        q = both[:, :BLOCK] + both[:, BLOCK:]
        hi = q.astype(BF16)
        lo = (q - hi.astype(F32)).astype(BF16)
        hi = jnp.concatenate([hi[j * tall:(j + 1) * tall] for j in range(blocks)], axis=1)
        lo = jnp.concatenate([lo[j * tall:(j + 1) * tall] for j in range(blocks)], axis=1)
        return jnp.dot(trow[t][:, :3 * tall], jnp.concatenate([hi, lo, hi], axis=0),
                       preferred_element_type=F32)

    own.wait()
    for i, (df, ds) in enumerate(DIRS):
        @pl.when(valid(-df, -ds))
        def _(i=i, df=df, ds=ds):
            sky_copy(i, df, ds).wait_recv()

    for p in range(planes + 2):
        beam = blur(skyh, p, p)
        r = iota(beam.shape, 0)
        outside = jnp.logical_or(jnp.logical_and(r == high - EDGE + HALF, si == ns - 1),
                                 jnp.logical_and(r == HALF + 1, si == 0))
        beam = jnp.where(outside, 0.0, beam)
        shifts = (shift_prev(beam), beam, shift_next(beam))
        for h in range(halves):
            bs[h, p] = jnp.concatenate(
                [x[h * EDGE:(h + 1) * EDGE] for x in shifts] + [jnp.zeros((8, length), F32)],
                axis=0).astype(BF16)

    for i, (df, ds) in enumerate(DIRS):
        @pl.when(valid(-df, -ds))
        def _(i=i, df=df, ds=ds):
            part_copy(i, df, ds).wait_recv()
    r = iota((rows, length), 0)
    for f in range(planes):
        total = part[f + 1, 0:rows]
        if f == 0:
            total = total + pf[0]
        if f == planes - 1:
            total = total + pf[1]
        for up in (0, 1):
            line = pe[2 + up, f + 1:f + 2]
            if f == 0:
                line = line + pe[4 + up, planes + 1:planes + 2]
            if f == planes - 1:
                line = line + pe[up, 0:1]
            total = total + jnp.where(r == (0 if up else rows - 1), line, 0.0)
        gbh[f, HALO:HALO + rows, PAD:PAD + length] = total.astype(BF16)
    for ds in (-1, 1):
        @pl.when(valid(0, ds))
        def _(ds=ds):
            gb_copy(ds).start()

    acc2 = jnp.zeros((3 * TALL3, wide), F32)
    for g in range(planes):
        for h in range(halves):
            acc2 = acc2 + lax.dot_general(
                bs[h, g:g + 3].reshape(3 * TALL3, length), cot_half(g, h),
                (((1,), (1,)), ((), ())), preferred_element_type=F32)
    lines = []
    for a in range(3):
        for b in range(3):
            for e in range(3):
                tile = acc2[a * TALL3 + e * EDGE:a * TALL3 + (e + 1) * EDGE]
                lines.append(jnp.sum(jnp.where(masks[b], tile, 0.0), axis=0, keepdims=True))
    lines.append(jnp.zeros((128 - 27, wide), F32))
    terms = lax.dot_general(member.astype(F32), jnp.concatenate(lines, axis=0),
                            (((1,), (1,)), ((), ())), precision=lax.Precision.HIGHEST,
                            preferred_element_type=F32)
    half = chans // 2
    packed = terms[:half] + pltpu.roll(terms[half:], 64, 1)
    mine[...] = packed
    slots[si] = packed

    def kg_copy(k, src, dst, send, recv, at, size, axis):
        to = lax.rem(at + k, size)
        return pltpu.make_async_remote_copy(
            src_ref=src, dst_ref=dst.at[at], send_sem=send.at[k], recv_sem=recv.at[k],
            device_id=(to, si) if axis == 0 else (fi, to), device_id_type=MESH)

    def kg_wait(k, src, dst, send, recv, at, size, axis):
        pltpu.make_async_remote_copy(
            src_ref=src, dst_ref=dst.at[lax.rem(at - k + size, size)], send_sem=send.at[k],
            recv_sem=recv.at[k], device_id=(fi, si), device_id_type=MESH).wait_recv()

    over_sky = (mine, slots, s_kg, r_kg, si, ns, 1)
    over_freq = (mine2, slots2, s_kf, r_kf, fi, nf, 0)
    for k in range(1, ns):
        kg_copy(k, *over_sky).start()

    for ds in (-1, 1):
        @pl.when(valid(0, -ds))
        def _(ds=ds):
            gb_copy(ds).wait_recv()

    out_copies = [pltpu.make_async_copy(outv.at[f], out_ref.at[f], out_sem.at[f])
                  for f in range(planes)]

    def finish(f):
        both = blur(gbh, f, f + 1)
        for h in range(halves):
            outv[f, h * HALF:(h + 1) * HALF] = both[h * EDGE:h * EDGE + HALF]
        out_copies[f].start()

    for f in range(planes // 2):
        finish(f)
    for k in range(1, ns):
        kg_wait(k, *over_sky)
    total = slots[0]
    for k in range(1, ns):
        total = total + slots[k]
    mine2[...] = total
    slots2[fi] = total
    for k in range(1, nf):
        kg_copy(k, *over_freq).start()
    for f in range(planes // 2, planes):
        finish(f)
    for k in range(1, nf):
        kg_wait(k, *over_freq)
    total = slots2[0]
    for k in range(1, nf):
        total = total + slots2[k]
    kg_ref[...] = total * scale

    for copy in out_copies:
        copy.wait()
    for i, (df, ds) in enumerate(DIRS):
        @pl.when(valid(df, ds))
        def _(i=i, df=df, ds=ds):
            sky_copy(i, df, ds).wait_send()
            part_copy(i, df, ds).wait_send()
            if ds == 0:
                hw_copy(df).wait_send()
            if df == 0:
                gb_copy(ds).wait_send()
    for k in range(1, ns):
        kg_copy(k, *over_sky).wait_send()
    for k in range(1, nf):
        kg_copy(k, *over_freq).wait_send()


def hand_on(sky_ref, packed_ref, out_ref, kg_ref, sems):
    copies = [pltpu.make_async_copy(sky_ref.at[f], out_ref.at[f], sems.at[f])
              for f in range(sky_ref.shape[0])]
    for copy in copies:
        copy.start()
    packed = packed_ref[...]
    half = packed.shape[0]
    kg_ref[0:half] = packed[:, :27]
    kg_ref[half:] = pltpu.roll(packed, 64, 1)[:, :27]
    for copy in copies:
        copy.wait()


def per_device(sky_cube, half_width, conv_weight, out_cotangent):
    planes, rows, length = sky_cube.shape
    chans = conv_weight.shape[0]
    nf, ns = lax.axis_size("freq"), lax.axis_size("sky")
    scale = 1.0 / math.sqrt(planes * nf * rows * ns * length)
    tall = rows + 2 * HALO
    wide = chans * HALF
    halves = rows // HALF
    high = halves * EDGE
    dma = pltpu.SemaphoreType.DMA

    def kernel(*refs):
        body(nf, ns, scale, *refs)

    sky_grad, packed = pl.pallas_call(
        kernel,
        out_shape=(jax.ShapeDtypeStruct((planes, rows, length), F32),
                   jax.ShapeDtypeStruct((chans // 2, 128), F32)),
        in_specs=[pl.BlockSpec(memory_space=pltpu.HBM)] * 4,
        out_specs=(pl.BlockSpec(memory_space=pltpu.HBM), pl.BlockSpec(memory_space=pltpu.VMEM)),
        scratch_shapes=[
            pltpu.VMEM((planes, rows, length), F32), dma((planes,)),
            pltpu.SMEM((planes,), jnp.int32),
            pltpu.VMEM((chans, 27), BF16),
            pltpu.VMEM((planes + 2, tall, length + 2 * PAD), BF16),
            pltpu.VMEM((planes, tall, length + 2 * PAD), BF16),
            pltpu.VMEM((planes, chans, rows, length), BF16),
            pltpu.VMEM((9 * EDGE + 8, wide), BF16),
            pltpu.VMEM((planes + 2, halves, 3, EDGE, length), F32),
            pltpu.VMEM((planes + 2, rows, length), F32),
            pltpu.VMEM((8, length), F32),
            pltpu.VMEM((8, length), F32),
            pltpu.VMEM((2, rows, length), F32),
            pltpu.VMEM((6, 8, length), F32),
            pltpu.VMEM((halves, planes + 2, TALL3, length), BF16),
            pltpu.VMEM((planes + 2, 3 * BLOCK, 2 * BLOCK), BF16),
            pltpu.VMEM((planes + 2, high, 256), BF16),
            pltpu.VMEM((planes + 2, 8, 256), F32),
            pltpu.VMEM((chans // 2, 128), F32),
            pltpu.VMEM((ns, chans // 2, 128), F32),
            pltpu.VMEM((chans // 2, 128), F32),
            pltpu.VMEM((nf, chans // 2, 128), F32),
            dma((planes,)), dma((3,)),
            dma((8,)), dma((8,)), dma((2,)), dma((2,)), dma((8,)), dma((8,)), dma((2,)), dma((2,)),
            dma((ns,)), dma((ns,)), dma((nf,)), dma((nf,)),
        ],
        compiler_params=pltpu.CompilerParams(
            collective_id=0, has_side_effects=True, vmem_limit_bytes=60 * 1024 * 1024),
        name="beam_backward",
    )(half_width, sky_cube, conv_weight, out_cotangent)
    return pl.pallas_call(
        hand_on,
        out_shape=(jax.ShapeDtypeStruct((planes, rows, length), F32),
                   jax.ShapeDtypeStruct((chans, 27), F32)),
        in_specs=[pl.BlockSpec(memory_space=pltpu.HBM), pl.BlockSpec(memory_space=pltpu.VMEM)],
        out_specs=(pl.BlockSpec(memory_space=pltpu.HBM), pl.BlockSpec(memory_space=pltpu.VMEM)),
        scratch_shapes=[dma((planes,))],
        compiler_params=pltpu.CompilerParams(vmem_limit_bytes=60 * 1024 * 1024),
        name="hand_on",
    )(sky_grad, packed)


def solution(mesh):
    return jax.shard_map(
        per_device,
        mesh=mesh,
        in_specs=(P("freq", "sky", None), P("freq"), P(), P(None, "freq", "sky", None)),
        out_specs=(P("freq", "sky", None), P()),
        check_vma=False,
    )
```

```python
import math

import jax
import jax.numpy as jnp
from jax import lax
from jax.experimental import pallas as pl
from jax.experimental.pallas import tpu as pltpu
from jax.sharding import PartitionSpec as P

MAXH = 12
HALO = 16
PAD = 128
BLOCK = 128
HALF = 16
EDGE = 24
TALL3 = 80
F32 = jnp.float32
BF16 = jnp.bfloat16
MESH = pl.DeviceIdType.MESH
DIRS = [(df, ds) for df in (-1, 0, 1) for ds in (-1, 0, 1) if (df, ds) != (0, 0)]


def iota(shape, dim):
    return lax.broadcasted_iota(jnp.int32, shape, dim)


def row_of(r, rows):
    return jnp.where(r <= rows, r, jnp.where(r == rows + 1, -1, -1000))


def band_mask(b, height, rows, width):
    shape = (height, width)
    return row_of(iota(shape, 0), rows) == lax.rem(iota(shape, 1), rows) + (b - 1)


def shift_next(x):
    n = x.shape[-1]
    return jnp.where(iota(x.shape, 1) == n - 1, 0.0, pltpu.roll(x, n - 1, 1))


def shift_prev(x):
    n = x.shape[-1]
    return jnp.where(iota(x.shape, 1) == 0, 0.0, pltpu.roll(x, 1, 1))


def body(nf, ns, scale, hw_hbm, sky_ref, w_hbm, cot_ref, out_ref, kg_ref,
         outv, out_sem, hw_ref, w_ref, skyh, gbh, cotv, bmat, acc, part, eu, ed, pf, pe, pc,
         bm, bs, tcol, trow, hwb, mine, slots, mine2, slots2,
         cot_sem, own_sem, s_sky, r_sky, s_part, r_part, s_gb, r_gb, s_bm, r_bm,
         s_kg, r_kg, s_kf, r_kf):
    planes, rows, length = out_ref.shape
    chans = w_ref.shape[0]
    wide = chans * HALF
    halves = rows // HALF
    high = halves * EDGE
    tall = rows + 2 * HALO
    fi, si = lax.axis_index("freq"), lax.axis_index("sky")

    def valid(df, ds):
        ok = None
        for at, step, size in ((fi, df, nf), (si, ds, ns)):
            if step:
                one = at + step < size if step > 0 else at + step >= 0
                ok = one if ok is None else jnp.logical_and(ok, one)
        return ok

    def span(step, own_lo, own_n, halo_n, full_n):
        if step == 0:
            return own_lo, 0, own_n
        if step > 0:
            return own_lo - halo_n, own_n - halo_n, halo_n
        return own_lo + own_n, 0, halo_n

    lanes = pl.ds(PAD, length)
    order = [0, planes - 1] + list(range(1, planes - 1))

    own_w = pltpu.make_async_copy(w_hbm, w_ref, own_sem.at[1])
    own_w.start()
    own_hw = pltpu.make_async_copy(hw_hbm, hw_ref, own_sem.at[2])
    own_hw.start()
    cot_copies = [pltpu.make_async_copy(cot_ref.at[:, g], cotv.at[g], cot_sem.at[g])
                  for g in range(planes)]
    for copy in cot_copies:
        copy.start()
    own = pltpu.make_async_copy(
        sky_ref, skyh.at[:, pl.ds(HALO, rows), lanes], own_sem.at[0])
    own.start()

    for df, ds in DIRS:
        @pl.when(jnp.logical_not(valid(-df, -ds)))
        def _(df=df, ds=ds):
            if df == 0:
                r0, _, rn = span(ds, HALO, rows, HALO, tall)
                zero = jnp.zeros((planes, rn, length), BF16)
                skyh[:, r0:r0 + rn, PAD:PAD + length] = zero
                gbh[:, r0:r0 + rn, PAD:PAD + length] = zero
                pe[0 if ds < 0 else 1] = jnp.zeros((planes, 8, length // 8), F32)
            elif ds == 0:
                bm[0 if df > 0 else planes + 1] = jnp.zeros((high, length), BF16)
                pf[0 if df > 0 else 1] = jnp.zeros((rows, length), F32)
            else:
                pc[(df > 0) * 2 + (ds > 0)] = jnp.zeros((1, 8, length // 8), F32)

    barrier = pltpu.get_barrier_semaphore()
    for k in range(1, ns):
        pl.semaphore_signal(barrier, inc=1, device_id=(fi, lax.rem(si + k, ns)), device_id_type=MESH)
    for k in range(1, nf):
        pl.semaphore_signal(barrier, inc=1, device_id=(lax.rem(fi + k, nf), si), device_id_type=MESH)
    greeted = jnp.int32(ns + nf - 2)
    for df, ds in DIRS:
        if df and ds:
            ok = valid(df, ds)
            greeted = greeted + jnp.where(ok, 1, 0)

            @pl.when(ok)
            def _(df=df, ds=ds):
                pl.semaphore_signal(barrier, inc=1, device_id=(fi + df, si + ds), device_id_type=MESH)

    for ref in (skyh, gbh):
        n = ref.shape[0]
        ref[:, :, 0:PAD] = jnp.zeros((n, tall, PAD), BF16)
        ref[:, :, PAD + length:] = jnp.zeros((n, tall, PAD), BF16)
    own_hw.wait()
    for k in range(planes):
        hwb[k] = jnp.full((8, 256), hw_ref[k].astype(F32))
    own_w.wait()
    member = (lax.div(iota((chans, wide), 1), HALF) == iota((chans, wide), 0))
    spread = lax.dot_general(w_ref[...], member.astype(BF16), (((0,), (0,)), ((), ())),
                             preferred_element_type=F32)
    masks = [band_mask(b, EDGE, HALF, wide) for b in range(3)]
    tiles = []
    for a in range(3):
        for e in range(3):
            tile = jnp.zeros((EDGE, wide), F32)
            for b in range(3):
                k = 9 * a + 3 * b + e
                tile = tile + jnp.where(masks[b], spread[k:k + 1, :], 0.0)
            tiles.append(tile)
    tiles.append(jnp.zeros((8, wide), F32))
    bmat[...] = jnp.concatenate(tiles, axis=0).astype(BF16)

    pl.semaphore_wait(barrier, greeted)

    def remote(src, dst, send, recv, df, ds):
        return pltpu.make_async_remote_copy(
            src_ref=src, dst_ref=dst, send_sem=send, recv_sem=recv,
            device_id=(fi + df, si + ds), device_id_type=MESH)

    def halo_copy(ref, send, recv, ds, f):
        i = (ds > 0) * planes + f
        r0, r1, rn = span(ds, HALO, rows, HALO, tall)
        return remote(ref.at[f, pl.ds(HALO + r1, rn), lanes], ref.at[f, pl.ds(r0, rn), lanes],
                      send.at[i], recv.at[i], 0, ds)

    def sky_copy(ds, f):
        return halo_copy(skyh, s_sky, r_sky, ds, f)

    def gb_copy(ds, f):
        return halo_copy(gbh, s_gb, r_gb, ds, f)

    def bm_copy(df):
        j = 0 if df > 0 else 1
        return remote(bm.at[planes if df > 0 else 1], bm.at[0 if df > 0 else planes + 1],
                      s_bm.at[j], r_bm.at[j], df, 0)

    def part_copy(i, df, ds):
        edge = ed if ds > 0 else eu
        if ds == 0:
            src, dst = part.at[planes + 1 if df > 0 else 0], pf.at[0 if df > 0 else 1]
        elif df == 0:
            src, dst = edge.at[pl.ds(1, planes)], pe.at[0 if ds < 0 else 1]
        else:
            src = edge.at[pl.ds(planes + 1 if df > 0 else 0, 1)]
            dst = pc.at[(df > 0) * 2 + (ds > 0)]
        return remote(src, dst, s_part.at[i], r_part.at[i], df, ds)

    own.wait()
    for ds in (-1, 1):
        @pl.when(valid(0, ds))
        def _(ds=ds):
            for f in order:
                sky_copy(ds, f).start()

    def cot_half(g, h):
        return cotv[g, :, h * HALF:(h + 1) * HALF, :].reshape(wide, length)

    def close_plane(p):
        r = iota((HALF, length), 0)
        piece = [acc[p, h, 1] + shift_next(acc[p, h, 0]) + shift_prev(acc[p, h, 2])
                 for h in range(halves)]
        for h in range(halves):
            total = piece[h][:HALF]
            if h > 0:
                total = total + jnp.where(r == 0, piece[h - 1][HALF:HALF + 1], 0.0)
            if h < halves - 1:
                total = total + jnp.where(r == HALF - 1, piece[h + 1][HALF + 1:HALF + 2], 0.0)
            part[p, h * HALF:(h + 1) * HALF] = total
        for ref, line in ((ed, piece[-1][HALF:HALF + 1]), (eu, piece[0][HALF + 1:HALF + 2])):
            n = length // 8
            ref[p] = jnp.concatenate([line[:, j * n:(j + 1) * n] for j in range(8)], axis=0)

    for g in range(planes):
        cot_copies[g].wait()
        for h in range(halves):
            res = jnp.dot(bmat[...], cot_half(g, h), preferred_element_type=F32)
            for a in range(3):
                piece = res[3 * a * EDGE:3 * (a + 1) * EDGE].reshape(3, EDGE, length)
                if g == 0 or a == 2:
                    acc[g + a, h] = piece
                else:
                    acc[g + a, h] += piece
        close_plane(g)
    close_plane(planes)
    close_plane(planes + 1)
    for i, (df, ds) in enumerate(DIRS):
        @pl.when(valid(df, ds))
        def _(i=i, df=df, ds=ds):
            part_copy(i, df, ds).start()

    def make_taps(p):
        h = hwb[p]
        h2 = h * h

        def profile(d, reach, reach2):
            d = d.astype(F32)
            return jnp.where(jnp.abs(d) <= reach, jnp.exp(-2.0 * (d * d) / reach2), 0.0)

        lane = iota((8, 256), 1)
        small = jnp.where(lane <= 2 * MAXH, profile(lane - MAXH, h, h2), 0.0)
        inv = 1.0 / jnp.sqrt(jnp.sum(small * small, axis=1, keepdims=True))
        inv = jnp.broadcast_to(inv, (8, 256))[0:1]
        h, h2 = h[0:1], h2[0:1]
        shape = (3 * BLOCK, BLOCK)
        val = profile(iota(shape, 0) - BLOCK - iota(shape, 1), h[:, :BLOCK], h2[:, :BLOCK]) * inv[:, :BLOCK]
        hi = val.astype(BF16)
        tcol[p, :, 0:BLOCK] = hi
        tcol[p, :, BLOCK:] = (val - hi.astype(F32)).astype(BF16)
        shape = (high, 256)
        lane = iota(shape, 1)
        row = row_of(lax.rem(iota(shape, 0), EDGE), HALF) + HALF * lax.div(iota(shape, 0), EDGE)
        val = profile(lax.rem(lane, tall) - HALO - row, h, h2) * inv
        hi = val.astype(BF16).astype(F32)
        trow[p] = jnp.where(lane < 2 * tall, hi, val - hi).astype(BF16)

    for p in range(planes):
        make_taps(p)

    def blur(src, p, t):
        blocks = length // BLOCK
        field = jnp.concatenate(
            [src[p, :, j * BLOCK:(j + 3) * BLOCK] for j in range(blocks)], axis=0)
        both = jnp.dot(field, tcol[t], preferred_element_type=F32)
        q = both[:, :BLOCK] + both[:, BLOCK:]
        hi = q.astype(BF16)
        lo = (q - hi.astype(F32)).astype(BF16)
        hi = jnp.concatenate([hi[j * tall:(j + 1) * tall] for j in range(blocks)], axis=1)
        lo = jnp.concatenate([lo[j * tall:(j + 1) * tall] for j in range(blocks)], axis=1)
        return jnp.dot(trow[t][:, :3 * tall], jnp.concatenate([hi, lo, hi], axis=0),
                       preferred_element_type=F32)

    for i, (df, ds) in enumerate(DIRS):
        @pl.when(valid(-df, -ds))
        def _(i=i, df=df, ds=ds):
            part_copy(i, df, ds).wait_recv()
    r = iota((rows, length), 0)
    for f in order:
        total = part[f + 1]
        if f == 0:
            total = total + pf[0]
        if f == planes - 1:
            total = total + pf[1]
        for up in (0, 1):
            line = pe[up, f]
            if f == 0:
                line = line + pc[2 + up, 0]
            if f == planes - 1:
                line = line + pc[up, 0]
            line = jnp.concatenate([line[k:k + 1] for k in range(8)], axis=1)
            total = total + jnp.where(r == (0 if up else rows - 1), line, 0.0)
        gbh[f, HALO:HALO + rows, PAD:PAD + length] = total.astype(BF16)
    for ds in (-1, 1):
        @pl.when(valid(0, ds))
        def _(ds=ds):
            for f in order:
                gb_copy(ds, f).start()

    def spread_beam(p, beam):
        shifts = (shift_prev(beam), beam, shift_next(beam))
        for h in range(halves):
            bs[h, p] = jnp.concatenate(
                [x[h * EDGE:(h + 1) * EDGE] for x in shifts] + [jnp.zeros((8, length), F32)],
                axis=0).astype(BF16)

    def wait_halo(make, f):
        for ds in (-1, 1):
            @pl.when(valid(0, -ds))
            def _(ds=ds):
                make(ds, f).wait_recv()

    for f in order:
        wait_halo(sky_copy, f)
        beam = blur(skyh, f, f)
        r = iota(beam.shape, 0)
        outside = jnp.logical_or(jnp.logical_and(r == high - EDGE + HALF, si == ns - 1),
                                 jnp.logical_and(r == HALF + 1, si == 0))
        beam = jnp.where(outside, 0.0, beam)
        if f in (0, planes - 1):
            bm[f + 1] = beam.astype(BF16)
            for df in (-1, 1):
                if f == (planes - 1 if df > 0 else 0):
                    @pl.when(valid(df, 0))
                    def _(df=df):
                        bm_copy(df).start()
        spread_beam(f + 1, beam)

    acc2 = jnp.zeros((3 * TALL3, wide), F32)
    for g in list(range(1, planes - 1)) + [0, planes - 1]:
        if g in (0, planes - 1):
            df = 1 if g == 0 else -1

            @pl.when(valid(-df, 0))
            def _(df=df):
                bm_copy(df).wait_recv()
            p = 0 if g == 0 else planes + 1
            spread_beam(p, bm[p].astype(F32))
        for h in range(halves):
            acc2 = acc2 + lax.dot_general(
                bs[h, g:g + 3].reshape(3 * TALL3, length), cot_half(g, h),
                (((1,), (1,)), ((), ())), preferred_element_type=F32)
    lines = []
    for a in range(3):
        for b in range(3):
            for e in range(3):
                tile = acc2[a * TALL3 + e * EDGE:a * TALL3 + (e + 1) * EDGE]
                lines.append(jnp.sum(jnp.where(masks[b], tile, 0.0), axis=0, keepdims=True))
    lines.append(jnp.zeros((128 - 27, wide), F32))
    terms = lax.dot_general(member.astype(F32), jnp.concatenate(lines, axis=0),
                            (((1,), (1,)), ((), ())), precision=lax.Precision.HIGHEST,
                            preferred_element_type=F32)
    half = chans // 2
    packed = terms[:half] + pltpu.roll(terms[half:], 64, 1)
    mine[...] = packed
    slots[si] = packed

    def kg_copy(k, src, dst, send, recv, at, size, axis):
        to = lax.rem(at + k, size)
        return pltpu.make_async_remote_copy(
            src_ref=src, dst_ref=dst.at[at], send_sem=send.at[k], recv_sem=recv.at[k],
            device_id=(to, si) if axis == 0 else (fi, to), device_id_type=MESH)

    def kg_wait(k, src, dst, send, recv, at, size, axis):
        pltpu.make_async_remote_copy(
            src_ref=src, dst_ref=dst.at[lax.rem(at - k + size, size)], send_sem=send.at[k],
            recv_sem=recv.at[k], device_id=(fi, si), device_id_type=MESH).wait_recv()

    over_sky = (mine, slots, s_kg, r_kg, si, ns, 1)
    over_freq = (mine2, slots2, s_kf, r_kf, fi, nf, 0)
    for k in range(1, ns):
        kg_copy(k, *over_sky).start()

    out_copies = [pltpu.make_async_copy(outv.at[f], out_ref.at[f], out_sem.at[f])
                  for f in range(planes)]

    def finish(f):
        wait_halo(gb_copy, f)
        both = blur(gbh, f, f)
        for h in range(halves):
            outv[f, h * HALF:(h + 1) * HALF] = both[h * EDGE:h * EDGE + HALF]
        out_copies[f].start()

    for f in order[:planes // 2]:
        finish(f)
    for k in range(1, ns):
        kg_wait(k, *over_sky)
    total = slots[0]
    for k in range(1, ns):
        total = total + slots[k]
    mine2[...] = total
    slots2[fi] = total
    for k in range(1, nf):
        kg_copy(k, *over_freq).start()
    for f in order[planes // 2:]:
        finish(f)
    for k in range(1, nf):
        kg_wait(k, *over_freq)
    total = slots2[0]
    for k in range(1, nf):
        total = total + slots2[k]
    kg_ref[...] = total * scale

    for copy in out_copies:
        copy.wait()
    for i, (df, ds) in enumerate(DIRS):
        @pl.when(valid(df, ds))
        def _(i=i, df=df, ds=ds):
            part_copy(i, df, ds).wait_send()
            if ds == 0:
                bm_copy(df).wait_send()
            if df == 0:
                for f in range(planes):
                    sky_copy(ds, f).wait_send()
                    gb_copy(ds, f).wait_send()
    for k in range(1, ns):
        kg_copy(k, *over_sky).wait_send()
    for k in range(1, nf):
        kg_copy(k, *over_freq).wait_send()


def hand_on(sky_ref, packed_ref, out_ref, kg_ref):
    out_ref[...] = sky_ref[...]

    @pl.when(pl.program_id(0) == 0)
    def _():
        packed = packed_ref[...]
        half = packed.shape[0]
        kg_ref[0:half] = packed[:, :27]
        kg_ref[half:] = pltpu.roll(packed, 64, 1)[:, :27]


def per_device(sky_cube, half_width, conv_weight, out_cotangent):
    planes, rows, length = sky_cube.shape
    chans = conv_weight.shape[0]
    nf, ns = lax.axis_size("freq"), lax.axis_size("sky")
    scale = 1.0 / math.sqrt(planes * nf * rows * ns * length)
    tall = rows + 2 * HALO
    wide = chans * HALF
    halves = rows // HALF
    high = halves * EDGE
    dma = pltpu.SemaphoreType.DMA

    def kernel(*refs):
        body(nf, ns, scale, *refs)

    sky_grad, packed = pl.pallas_call(
        kernel,
        out_shape=(jax.ShapeDtypeStruct((planes, rows, length), F32),
                   jax.ShapeDtypeStruct((chans // 2, 128), F32)),
        in_specs=[pl.BlockSpec(memory_space=pltpu.HBM)] * 4,
        out_specs=(pl.BlockSpec(memory_space=pltpu.HBM), pl.BlockSpec(memory_space=pltpu.VMEM)),
        scratch_shapes=[
            pltpu.VMEM((planes, rows, length), F32), dma((planes,)),
            pltpu.SMEM((planes,), jnp.int32),
            pltpu.VMEM((chans, 27), BF16),
            pltpu.VMEM((planes, tall, length + 2 * PAD), BF16),
            pltpu.VMEM((planes, tall, length + 2 * PAD), BF16),
            pltpu.VMEM((planes, chans, rows, length), BF16),
            pltpu.VMEM((9 * EDGE + 8, wide), BF16),
            pltpu.VMEM((planes + 2, halves, 3, EDGE, length), F32),
            pltpu.VMEM((planes + 2, rows, length), F32),
            pltpu.VMEM((planes + 2, 8, length // 8), F32),
            pltpu.VMEM((planes + 2, 8, length // 8), F32),
            pltpu.VMEM((2, rows, length), F32),
            pltpu.VMEM((2, planes, 8, length // 8), F32),
            pltpu.VMEM((4, 1, 8, length // 8), F32),
            pltpu.VMEM((planes + 2, high, length), BF16),
            pltpu.VMEM((halves, planes + 2, TALL3, length), BF16),
            pltpu.VMEM((planes, 3 * BLOCK, 2 * BLOCK), BF16),
            pltpu.VMEM((planes, high, 256), BF16),
            pltpu.VMEM((planes, 8, 256), F32),
            pltpu.VMEM((chans // 2, 128), F32),
            pltpu.VMEM((ns, chans // 2, 128), F32),
            pltpu.VMEM((chans // 2, 128), F32),
            pltpu.VMEM((nf, chans // 2, 128), F32),
            dma((planes,)), dma((3,)),
            dma((2 * planes,)), dma((2 * planes,)), dma((8,)), dma((8,)),
            dma((2 * planes,)), dma((2 * planes,)), dma((2,)), dma((2,)),
            dma((ns,)), dma((ns,)), dma((nf,)), dma((nf,)),
        ],
        compiler_params=pltpu.CompilerParams(
            collective_id=0, has_side_effects=True, vmem_limit_bytes=60 * 1024 * 1024),
        name="beam_backward",
    )(half_width, sky_cube, conv_weight, out_cotangent)
    return pl.pallas_call(
        hand_on,
        out_shape=(jax.ShapeDtypeStruct((planes, rows, length), F32),
                   jax.ShapeDtypeStruct((chans, 27), F32)),
        grid=(2,),
        in_specs=[pl.BlockSpec((planes // 2, rows, length), lambda f: (f, 0, 0)),
                  pl.BlockSpec((chans // 2, 128), lambda f: (0, 0))],
        out_specs=(pl.BlockSpec((planes // 2, rows, length), lambda f: (f, 0, 0)),
                   pl.BlockSpec((chans, 27), lambda f: (0, 0))),
        compiler_params=pltpu.CompilerParams(vmem_limit_bytes=60 * 1024 * 1024),
        name="hand_on",
    )(sky_grad, packed)


def solution(mesh):
    return jax.shard_map(
        per_device,
        mesh=mesh,
        in_specs=(P("freq", "sky", None), P("freq"), P(), P(None, "freq", "sky", None)),
        out_specs=(P("freq", "sky", None), P()),
        check_vma=False,
    )
```

```python
import math

import jax
import jax.numpy as jnp
from jax import lax
from jax.experimental import pallas as pl
from jax.experimental.pallas import tpu as pltpu
from jax.sharding import PartitionSpec as P

MAXH = 12
HALO = 16
PAD = 128
BLOCK = 128
HALF = 16
EDGE = 24
TALL3 = 80
F32 = jnp.float32
BF16 = jnp.bfloat16
MESH = pl.DeviceIdType.MESH
DIRS = [(df, ds) for df in (-1, 0, 1) for ds in (-1, 0, 1) if (df, ds) != (0, 0)]


def iota(shape, dim):
    return lax.broadcasted_iota(jnp.int32, shape, dim)


def row_of(r, rows):
    return jnp.where(r <= rows, r, jnp.where(r == rows + 1, -1, -1000))


def band_mask(b, height, rows, width):
    shape = (height, width)
    return row_of(iota(shape, 0), rows) == lax.rem(iota(shape, 1), rows) + (b - 1)


def shift_next(x):
    n = x.shape[-1]
    return jnp.where(iota(x.shape, 1) == n - 1, 0.0, pltpu.roll(x, n - 1, 1))


def shift_prev(x):
    n = x.shape[-1]
    return jnp.where(iota(x.shape, 1) == 0, 0.0, pltpu.roll(x, 1, 1))


def body(nf, ns, scale, hw_hbm, sky_ref, w_hbm, cot_ref, out_ref, kg_ref,
         outv, out_sem, hw_ref, w_ref, skyh, gbh, cotv, bmat, acc, part, eu, ed, pf, pe, pc,
         bm, bs, tcol, trow, hwb, mine, slots, mine2, slots2,
         cot_sem, own_sem, s_sky, r_sky, s_part, r_part, s_gb, r_gb, s_bm, r_bm,
         s_kg, r_kg, s_kf, r_kf):
    planes, rows, length = out_ref.shape
    chans = w_ref.shape[0]
    wide = chans * HALF
    halves = rows // HALF
    high = halves * EDGE
    tall = rows + 2 * HALO
    fi, si = lax.axis_index("freq"), lax.axis_index("sky")

    def valid(df, ds):
        ok = None
        for at, step, size in ((fi, df, nf), (si, ds, ns)):
            if step:
                one = at + step < size if step > 0 else at + step >= 0
                ok = one if ok is None else jnp.logical_and(ok, one)
        return ok

    def span(step, own_lo, own_n, halo_n, full_n):
        if step == 0:
            return own_lo, 0, own_n
        if step > 0:
            return own_lo - halo_n, own_n - halo_n, halo_n
        return own_lo + own_n, 0, halo_n

    lanes = pl.ds(PAD, length)
    order = [0, planes - 1] + list(range(1, planes - 1))
    pairs = [order[k:k + 2] for k in range(0, planes, 2)]

    own_w = pltpu.make_async_copy(w_hbm, w_ref, own_sem.at[1])
    own_w.start()
    own_hw = pltpu.make_async_copy(hw_hbm, hw_ref, own_sem.at[2])
    own_hw.start()
    cot_copies = [pltpu.make_async_copy(cot_ref.at[:, g], cotv.at[g], cot_sem.at[g])
                  for g in range(planes)]
    for copy in cot_copies:
        copy.start()
    own = pltpu.make_async_copy(
        sky_ref, skyh.at[:, pl.ds(HALO, rows), lanes], own_sem.at[0])
    own.start()

    for df, ds in DIRS:
        @pl.when(jnp.logical_not(valid(-df, -ds)))
        def _(df=df, ds=ds):
            if df == 0:
                r0, _, rn = span(ds, HALO, rows, HALO, tall)
                zero = jnp.zeros((planes, rn, length), BF16)
                skyh[:, r0:r0 + rn, PAD:PAD + length] = zero
                gbh[:, r0:r0 + rn, PAD:PAD + length] = zero
                pe[0 if ds < 0 else 1] = jnp.zeros((planes, 8, length // 8), F32)
            elif ds == 0:
                bm[0 if df > 0 else planes + 1] = jnp.zeros((high, length), BF16)
                pf[0 if df > 0 else 1] = jnp.zeros((rows, length), F32)
            else:
                pc[(df > 0) * 2 + (ds > 0)] = jnp.zeros((1, 8, length // 8), F32)

    barrier = pltpu.get_barrier_semaphore()
    for k in range(1, ns):
        pl.semaphore_signal(barrier, inc=1, device_id=(fi, lax.rem(si + k, ns)), device_id_type=MESH)
    for k in range(1, nf):
        pl.semaphore_signal(barrier, inc=1, device_id=(lax.rem(fi + k, nf), si), device_id_type=MESH)
    greeted = jnp.int32(ns + nf - 2)
    for df, ds in DIRS:
        if df and ds:
            ok = valid(df, ds)
            greeted = greeted + jnp.where(ok, 1, 0)

            @pl.when(ok)
            def _(df=df, ds=ds):
                pl.semaphore_signal(barrier, inc=1, device_id=(fi + df, si + ds), device_id_type=MESH)

    for ref in (skyh, gbh):
        n = ref.shape[0]
        ref[:, :, 0:PAD] = jnp.zeros((n, tall, PAD), BF16)
        ref[:, :, PAD + length:] = jnp.zeros((n, tall, PAD), BF16)
    own_hw.wait()
    for k in range(planes):
        hwb[k] = jnp.full((8, 256), hw_ref[k].astype(F32))
    own_w.wait()
    member = (lax.div(iota((chans, wide), 1), HALF) == iota((chans, wide), 0))
    spread = lax.dot_general(w_ref[...], member.astype(BF16), (((0,), (0,)), ((), ())),
                             preferred_element_type=F32)
    masks = [band_mask(b, EDGE, HALF, wide) for b in range(3)]
    tiles = []
    for a in range(3):
        for e in range(3):
            tile = jnp.zeros((EDGE, wide), F32)
            for b in range(3):
                k = 9 * a + 3 * b + e
                tile = tile + jnp.where(masks[b], spread[k:k + 1, :], 0.0)
            tiles.append(tile)
    tiles.append(jnp.zeros((8, wide), F32))
    bmat[...] = jnp.concatenate(tiles, axis=0).astype(BF16)

    pl.semaphore_wait(barrier, greeted)

    def remote(src, dst, send, recv, df, ds):
        return pltpu.make_async_remote_copy(
            src_ref=src, dst_ref=dst, send_sem=send, recv_sem=recv,
            device_id=(fi + df, si + ds), device_id_type=MESH)

    def halo_copy(ref, send, recv, ds, f):
        i = (ds > 0) * planes + f
        r0, r1, rn = span(ds, HALO, rows, HALO, tall)
        return remote(ref.at[f, pl.ds(HALO + r1, rn), lanes], ref.at[f, pl.ds(r0, rn), lanes],
                      send.at[i], recv.at[i], 0, ds)

    def sky_copy(ds, f):
        return halo_copy(skyh, s_sky, r_sky, ds, f)

    def gb_copy(ds, f):
        return halo_copy(gbh, s_gb, r_gb, ds, f)

    def bm_copy(df):
        j = 0 if df > 0 else 1
        return remote(bm.at[planes if df > 0 else 1], bm.at[0 if df > 0 else planes + 1],
                      s_bm.at[j], r_bm.at[j], df, 0)

    def part_copy(i, df, ds):
        edge = ed if ds > 0 else eu
        if ds == 0:
            src, dst = part.at[planes + 1 if df > 0 else 0], pf.at[0 if df > 0 else 1]
        elif df == 0:
            src, dst = edge.at[pl.ds(1, planes)], pe.at[0 if ds < 0 else 1]
        else:
            src = edge.at[pl.ds(planes + 1 if df > 0 else 0, 1)]
            dst = pc.at[(df > 0) * 2 + (ds > 0)]
        return remote(src, dst, s_part.at[i], r_part.at[i], df, ds)

    own.wait()
    for ds in (-1, 1):
        @pl.when(valid(0, ds))
        def _(ds=ds):
            for f in order:
                sky_copy(ds, f).start()

    def cot_half(g, h):
        return cotv[g, :, h * HALF:(h + 1) * HALF, :].reshape(wide, length)

    def close_plane(p):
        r = iota((HALF, length), 0)
        piece = [acc[p, h, 1] + shift_next(acc[p, h, 0]) + shift_prev(acc[p, h, 2])
                 for h in range(halves)]
        for h in range(halves):
            total = piece[h][:HALF]
            if h > 0:
                total = total + jnp.where(r == 0, piece[h - 1][HALF:HALF + 1], 0.0)
            if h < halves - 1:
                total = total + jnp.where(r == HALF - 1, piece[h + 1][HALF + 1:HALF + 2], 0.0)
            part[p, h * HALF:(h + 1) * HALF] = total
        for ref, line in ((ed, piece[-1][HALF:HALF + 1]), (eu, piece[0][HALF + 1:HALF + 2])):
            n = length // 8
            ref[p] = jnp.concatenate([line[:, j * n:(j + 1) * n] for j in range(8)], axis=0)

    for g in range(planes):
        cot_copies[g].wait()
        for h in range(halves):
            res = jnp.dot(bmat[...], cot_half(g, h), preferred_element_type=F32)
            for a in range(3):
                piece = res[3 * a * EDGE:3 * (a + 1) * EDGE].reshape(3, EDGE, length)
                if g == 0 or a == 2:
                    acc[g + a, h] = piece
                else:
                    acc[g + a, h] += piece
        close_plane(g)
    close_plane(planes)
    close_plane(planes + 1)
    for i, (df, ds) in enumerate(DIRS):
        @pl.when(valid(df, ds))
        def _(i=i, df=df, ds=ds):
            part_copy(i, df, ds).start()

    def make_taps(p):
        h = hwb[p]
        fall = -2.0 / (h * h)

        def profile(d, reach, fall):
            d = d.astype(F32)
            return jnp.where(jnp.abs(d) <= reach, jnp.exp((d * d) * fall), 0.0)

        lane = iota((8, 256), 1)
        small = jnp.where(lane <= 2 * MAXH, profile(lane - MAXH, h, fall), 0.0)
        inv = 1.0 / jnp.sqrt(jnp.sum(small * small, axis=1, keepdims=True))
        inv = jnp.broadcast_to(inv, (8, 256))[0:1]
        h, fall = h[0:1], fall[0:1]
        shape = (3 * BLOCK, BLOCK)
        val = profile(iota(shape, 0) - BLOCK - iota(shape, 1), h[:, :BLOCK], fall[:, :BLOCK]) * inv[:, :BLOCK]
        hi = val.astype(BF16)
        tcol[p, :, 0:BLOCK] = hi
        tcol[p, :, BLOCK:] = (val - hi.astype(F32)).astype(BF16)
        shape = (high, 4 * tall)
        lane = iota(shape, 1)
        row = row_of(lax.rem(iota(shape, 0), EDGE), HALF) + HALF * lax.div(iota(shape, 0), EDGE)
        val = profile(lax.rem(lane, tall) - HALO - row, h, fall) * inv
        hi = val.astype(BF16).astype(F32)
        at = lane - 2 * tall * (order.index(p) % 2)
        here = jnp.logical_and(at >= 0, at < 2 * tall)
        first = jnp.logical_and(at >= 0, at < tall)
        trow[p, 0:high] = jnp.where(here, hi, 0.0).astype(BF16)
        trow[p, high:] = jnp.where(first, val - hi, 0.0).astype(BF16)

    for p in range(planes):
        make_taps(p)

    def blur(src, pair):
        blocks = length // BLOCK
        parts = []
        for p in pair:
            field = jnp.concatenate(
                [src[p, :, j * BLOCK:(j + 3) * BLOCK] for j in range(blocks)], axis=0)
            both = jnp.dot(field, tcol[p], preferred_element_type=F32)
            q = both[:, :BLOCK] + both[:, BLOCK:]
            hi = q.astype(BF16)
            lo = (q - hi.astype(F32)).astype(BF16)
            for x in (hi, lo):
                parts.append(jnp.concatenate(
                    [x[j * tall:(j + 1) * tall] for j in range(blocks)], axis=1))
        left = jnp.concatenate([trow[p] for p in pair], axis=0)
        res = jnp.dot(left, jnp.concatenate(parts, axis=0), preferred_element_type=F32)
        return [res[2 * i * high:(2 * i + 1) * high] + res[(2 * i + 1) * high:(2 * i + 2) * high]
                for i in range(len(pair))]

    def spread_beam(p, beam):
        shifts = (shift_prev(beam), beam, shift_next(beam))
        for h in range(halves):
            bs[h, p] = jnp.concatenate(
                [x[h * EDGE:(h + 1) * EDGE] for x in shifts] + [jnp.zeros((8, length), F32)],
                axis=0).astype(BF16)

    def wait_halos(make, which):
        for ds in (-1, 1):
            @pl.when(valid(0, -ds))
            def _(ds=ds):
                for f in which:
                    make(ds, f).wait_recv()

    def make_beams(pair):
        beams = blur(skyh, pair)
        r = iota(beams[0].shape, 0)
        outside = jnp.logical_or(jnp.logical_and(r == high - EDGE + HALF, si == ns - 1),
                                 jnp.logical_and(r == HALF + 1, si == 0))
        for f, beam in zip(pair, beams):
            beam = jnp.where(outside, 0.0, beam)
            if f in (0, planes - 1):
                bm[f + 1] = beam.astype(BF16)
            spread_beam(f + 1, beam)

    wait_halos(sky_copy, order)
    make_beams(pairs[0])
    for df in (-1, 1):
        @pl.when(valid(df, 0))
        def _(df=df):
            bm_copy(df).start()

    for i, (df, ds) in enumerate(DIRS):
        @pl.when(valid(-df, -ds))
        def _(i=i, df=df, ds=ds):
            part_copy(i, df, ds).wait_recv()
    r = iota((rows, length), 0)
    for f in order:
        total = part[f + 1]
        if f == 0:
            total = total + pf[0]
        if f == planes - 1:
            total = total + pf[1]
        for up in (0, 1):
            line = pe[up, f]
            if f == 0:
                line = line + pc[2 + up, 0]
            if f == planes - 1:
                line = line + pc[up, 0]
            line = jnp.concatenate([line[k:k + 1] for k in range(8)], axis=1)
            total = total + jnp.where(r == (0 if up else rows - 1), line, 0.0)
        gbh[f, HALO:HALO + rows, PAD:PAD + length] = total.astype(BF16)
    for ds in (-1, 1):
        @pl.when(valid(0, ds))
        def _(ds=ds):
            for f in order:
                gb_copy(ds, f).start()

    for pair in pairs[1:]:
        make_beams(pair)

    acc2 = jnp.zeros((3 * TALL3, wide), F32)
    def gram(total, g):
        for h in range(halves):
            total = total + lax.dot_general(
                bs[h, g:g + 3].reshape(3 * TALL3, length), cot_half(g, h),
                (((1,), (1,)), ((), ())), preferred_element_type=F32)
        return total

    for g in range(1, planes - 1):
        acc2 = gram(acc2, g)
    for df in (-1, 1):
        @pl.when(valid(-df, 0))
        def _(df=df):
            bm_copy(df).wait_recv()
    for p in (0, planes + 1):
        spread_beam(p, bm[p].astype(F32))
    for g in (0, planes - 1):
        acc2 = gram(acc2, g)
    lines = []
    for a in range(3):
        for b in range(3):
            for e in range(3):
                tile = acc2[a * TALL3 + e * EDGE:a * TALL3 + (e + 1) * EDGE]
                lines.append(jnp.sum(jnp.where(masks[b], tile, 0.0), axis=0, keepdims=True))
    lines.append(jnp.zeros((128 - 27, wide), F32))
    terms = lax.dot_general(member.astype(F32), jnp.concatenate(lines, axis=0),
                            (((1,), (1,)), ((), ())), precision=lax.Precision.HIGHEST,
                            preferred_element_type=F32)
    half = chans // 2
    packed = terms[:half] + pltpu.roll(terms[half:], 64, 1)
    mine[...] = packed
    slots[si] = packed

    def kg_copy(k, src, dst, send, recv, at, size, axis):
        to = lax.rem(at + k, size)
        return pltpu.make_async_remote_copy(
            src_ref=src, dst_ref=dst.at[at], send_sem=send.at[k], recv_sem=recv.at[k],
            device_id=(to, si) if axis == 0 else (fi, to), device_id_type=MESH)

    def kg_wait(k, src, dst, send, recv, at, size, axis):
        pltpu.make_async_remote_copy(
            src_ref=src, dst_ref=dst.at[lax.rem(at - k + size, size)], send_sem=send.at[k],
            recv_sem=recv.at[k], device_id=(fi, si), device_id_type=MESH).wait_recv()

    over_sky = (mine, slots, s_kg, r_kg, si, ns, 1)
    over_freq = (mine2, slots2, s_kf, r_kf, fi, nf, 0)
    for k in range(1, ns):
        kg_copy(k, *over_sky).start()

    out_copies = [pltpu.make_async_copy(outv.at[f], out_ref.at[f], out_sem.at[f])
                  for f in range(planes)]

    def finish(pair):
        for f, both in zip(pair, blur(gbh, pair)):
            for h in range(halves):
                outv[f, h * HALF:(h + 1) * HALF] = both[h * EDGE:h * EDGE + HALF]
            out_copies[f].start()

    wait_halos(gb_copy, order)
    finish(pairs[0])
    for k in range(1, ns):
        kg_wait(k, *over_sky)
    total = slots[0]
    for k in range(1, ns):
        total = total + slots[k]
    mine2[...] = total
    slots2[fi] = total
    for k in range(1, nf):
        kg_copy(k, *over_freq).start()
    for pair in pairs[1:]:
        finish(pair)
    for k in range(1, nf):
        kg_wait(k, *over_freq)
    total = slots2[0]
    for k in range(1, nf):
        total = total + slots2[k]
    kg_ref[...] = total * scale

    for copy in out_copies:
        copy.wait()
    for i, (df, ds) in enumerate(DIRS):
        @pl.when(valid(df, ds))
        def _(i=i, df=df, ds=ds):
            part_copy(i, df, ds).wait_send()
            if ds == 0:
                bm_copy(df).wait_send()
            if df == 0:
                for f in range(planes):
                    sky_copy(ds, f).wait_send()
                    gb_copy(ds, f).wait_send()
    for k in range(1, ns):
        kg_copy(k, *over_sky).wait_send()
    for k in range(1, nf):
        kg_copy(k, *over_freq).wait_send()


def hand_on(sky_ref, packed_ref, out_ref, kg_ref):
    out_ref[...] = sky_ref[...]

    @pl.when(pl.program_id(0) == 0)
    def _():
        packed = packed_ref[...]
        half = packed.shape[0]
        kg_ref[0:half] = packed[:, :27]
        kg_ref[half:] = pltpu.roll(packed, 64, 1)[:, :27]


def per_device(sky_cube, half_width, conv_weight, out_cotangent):
    planes, rows, length = sky_cube.shape
    chans = conv_weight.shape[0]
    nf, ns = lax.axis_size("freq"), lax.axis_size("sky")
    scale = 1.0 / math.sqrt(planes * nf * rows * ns * length)
    tall = rows + 2 * HALO
    wide = chans * HALF
    halves = rows // HALF
    high = halves * EDGE
    dma = pltpu.SemaphoreType.DMA

    def kernel(*refs):
        body(nf, ns, scale, *refs)

    sky_grad, packed = pl.pallas_call(
        kernel,
        out_shape=(jax.ShapeDtypeStruct((planes, rows, length), F32),
                   jax.ShapeDtypeStruct((chans // 2, 128), F32)),
        in_specs=[pl.BlockSpec(memory_space=pltpu.HBM)] * 4,
        out_specs=(pl.BlockSpec(memory_space=pltpu.HBM), pl.BlockSpec(memory_space=pltpu.VMEM)),
        scratch_shapes=[
            pltpu.VMEM((planes, rows, length), F32), dma((planes,)),
            pltpu.SMEM((planes,), jnp.int32),
            pltpu.VMEM((chans, 27), BF16),
            pltpu.VMEM((planes, tall, length + 2 * PAD), BF16),
            pltpu.VMEM((planes, tall, length + 2 * PAD), BF16),
            pltpu.VMEM((planes, chans, rows, length), BF16),
            pltpu.VMEM((9 * EDGE + 8, wide), BF16),
            pltpu.VMEM((planes + 2, halves, 3, EDGE, length), F32),
            pltpu.VMEM((planes + 2, rows, length), F32),
            pltpu.VMEM((planes + 2, 8, length // 8), F32),
            pltpu.VMEM((planes + 2, 8, length // 8), F32),
            pltpu.VMEM((2, rows, length), F32),
            pltpu.VMEM((2, planes, 8, length // 8), F32),
            pltpu.VMEM((4, 1, 8, length // 8), F32),
            pltpu.VMEM((planes + 2, high, length), BF16),
            pltpu.VMEM((halves, planes + 2, TALL3, length), BF16),
            pltpu.VMEM((planes, 3 * BLOCK, 2 * BLOCK), BF16),
            pltpu.VMEM((planes, 2 * high, 4 * tall), BF16),
            pltpu.VMEM((planes, 8, 256), F32),
            pltpu.VMEM((chans // 2, 128), F32),
            pltpu.VMEM((ns, chans // 2, 128), F32),
            pltpu.VMEM((chans // 2, 128), F32),
            pltpu.VMEM((nf, chans // 2, 128), F32),
            dma((planes,)), dma((3,)),
            dma((2 * planes,)), dma((2 * planes,)), dma((8,)), dma((8,)),
            dma((2 * planes,)), dma((2 * planes,)), dma((2,)), dma((2,)),
            dma((ns,)), dma((ns,)), dma((nf,)), dma((nf,)),
        ],
        compiler_params=pltpu.CompilerParams(
            collective_id=0, has_side_effects=True, vmem_limit_bytes=60 * 1024 * 1024),
        name="beam_backward",
    )(half_width, sky_cube, conv_weight, out_cotangent)
    return pl.pallas_call(
        hand_on,
        out_shape=(jax.ShapeDtypeStruct((planes, rows, length), F32),
                   jax.ShapeDtypeStruct((chans, 27), F32)),
        grid=(2,),
        in_specs=[pl.BlockSpec((planes // 2, rows, length), lambda f: (f, 0, 0)),
                  pl.BlockSpec((chans // 2, 128), lambda f: (0, 0))],
        out_specs=(pl.BlockSpec((planes // 2, rows, length), lambda f: (f, 0, 0)),
                   pl.BlockSpec((chans, 27), lambda f: (0, 0))),
        compiler_params=pltpu.CompilerParams(vmem_limit_bytes=60 * 1024 * 1024),
        name="hand_on",
    )(sky_grad, packed)


def solution(mesh):
    return jax.shard_map(
        per_device,
        mesh=mesh,
        in_specs=(P("freq", "sky", None), P("freq"), P(), P(None, "freq", "sky", None)),
        out_specs=(P("freq", "sky", None), P()),
        check_vma=False,
    )
```

```python
import math

import jax
import jax.numpy as jnp
from jax import lax
from jax.experimental import pallas as pl
from jax.experimental.pallas import tpu as pltpu
from jax.sharding import PartitionSpec as P

MAXH = 12
HALO = 16
PAD = 128
BLOCK = 128
HALF = 16
EDGE = 24
TALL3 = 80
F32 = jnp.float32
BF16 = jnp.bfloat16
MESH = pl.DeviceIdType.MESH
DIRS = [(df, ds) for df in (-1, 0, 1) for ds in (-1, 0, 1) if (df, ds) != (0, 0)]


def iota(shape, dim):
    return lax.broadcasted_iota(jnp.int32, shape, dim)


def row_of(r, rows):
    return jnp.where(r <= rows, r, jnp.where(r == rows + 1, -1, -1000))


def band_mask(b, height, rows, width):
    shape = (height, width)
    return row_of(iota(shape, 0), rows) == lax.rem(iota(shape, 1), rows) + (b - 1)


def shift_next(x):
    n = x.shape[-1]
    return jnp.where(iota(x.shape, 1) == n - 1, 0.0, pltpu.roll(x, n - 1, 1))


def shift_prev(x):
    n = x.shape[-1]
    return jnp.where(iota(x.shape, 1) == 0, 0.0, pltpu.roll(x, 1, 1))


def body(nf, ns, scale, hw_hbm, sky_ref, w_hbm, cot_ref, out_ref, kg_ref,
         outv, out_sem, hw_ref, w_ref, skyh, gbh, gs, cotv, bmat, acc, part, eu, ed, pf, pe, pc,
         bm, bs, tcol, trow, hwb, mine, slots, mine2, slots2,
         cot_sem, own_sem, s_sky, r_sky, s_part, r_part, s_gb, r_gb, s_bm, r_bm,
         s_kg, r_kg, s_kf, r_kf):
    planes, rows, length = out_ref.shape
    chans = w_ref.shape[0]
    wide = chans * HALF
    halves = rows // HALF
    high = halves * EDGE
    tall = rows + 2 * HALO
    fi, si = lax.axis_index("freq"), lax.axis_index("sky")

    def valid(df, ds):
        ok = None
        for at, step, size in ((fi, df, nf), (si, ds, ns)):
            if step:
                one = at + step < size if step > 0 else at + step >= 0
                ok = one if ok is None else jnp.logical_and(ok, one)
        return ok

    def span(step, own_lo, own_n, halo_n, full_n):
        if step == 0:
            return own_lo, 0, own_n
        if step > 0:
            return own_lo - halo_n, own_n - halo_n, halo_n
        return own_lo + own_n, 0, halo_n

    lanes = pl.ds(PAD, length)
    order = [0, planes - 1] + list(range(1, planes - 1))
    pairs = [order[k:k + 2] for k in range(0, planes, 2)]

    own_w = pltpu.make_async_copy(w_hbm, w_ref, own_sem.at[1])
    own_w.start()
    own_hw = pltpu.make_async_copy(hw_hbm, hw_ref, own_sem.at[2])
    own_hw.start()
    cot_copies = [pltpu.make_async_copy(cot_ref.at[:, g], cotv.at[g], cot_sem.at[g])
                  for g in range(planes)]
    for copy in cot_copies:
        copy.start()
    own = pltpu.make_async_copy(
        sky_ref, skyh.at[:, pl.ds(HALO, rows), lanes], own_sem.at[0])
    own.start()

    for df, ds in DIRS:
        @pl.when(jnp.logical_not(valid(-df, -ds)))
        def _(df=df, ds=ds):
            if df == 0:
                r0, _, rn = span(ds, HALO, rows, HALO, tall)
                zero = jnp.zeros((planes, rn, length), BF16)
                skyh[:, r0:r0 + rn, PAD:PAD + length] = zero
                gbh[:, r0:r0 + rn, PAD:PAD + length] = zero
                pe[0 if ds < 0 else 1] = jnp.zeros((planes, 8, length // 8), F32)
            elif ds == 0:
                bm[0 if df > 0 else planes + 1] = jnp.zeros((high, length), BF16)
                pf[0 if df > 0 else 1] = jnp.zeros((rows, length), F32)
            else:
                pc[(df > 0) * 2 + (ds > 0)] = jnp.zeros((1, 8, length // 8), F32)

    barrier = pltpu.get_barrier_semaphore()
    for k in range(1, ns):
        pl.semaphore_signal(barrier, inc=1, device_id=(fi, lax.rem(si + k, ns)), device_id_type=MESH)
    for k in range(1, nf):
        pl.semaphore_signal(barrier, inc=1, device_id=(lax.rem(fi + k, nf), si), device_id_type=MESH)
    greeted = jnp.int32(ns + nf - 2)
    for df, ds in DIRS:
        if df and ds:
            ok = valid(df, ds)
            greeted = greeted + jnp.where(ok, 1, 0)

            @pl.when(ok)
            def _(df=df, ds=ds):
                pl.semaphore_signal(barrier, inc=1, device_id=(fi + df, si + ds), device_id_type=MESH)

    for ref in (skyh, gbh):
        n = ref.shape[0]
        ref[:, :, 0:PAD] = jnp.zeros((n, tall, PAD), BF16)
        ref[:, :, PAD + length:] = jnp.zeros((n, tall, PAD), BF16)
    own_hw.wait()
    for k in range(planes):
        hwb[k] = jnp.full((8, 256), hw_ref[k].astype(F32))
    own_w.wait()
    member = (lax.div(iota((chans, wide), 1), HALF) == iota((chans, wide), 0))
    spread = lax.dot_general(w_ref[...], member.astype(BF16), (((0,), (0,)), ((), ())),
                             preferred_element_type=F32)
    masks = [band_mask(b, EDGE, HALF, wide) for b in range(3)]
    tiles = []
    for a in range(3):
        for e in range(3):
            tile = jnp.zeros((EDGE, wide), F32)
            for b in range(3):
                k = 9 * a + 3 * b + e
                tile = tile + jnp.where(masks[b], spread[k:k + 1, :], 0.0)
            tiles.append(tile)
    tiles.append(jnp.zeros((8, wide), F32))
    bmat[...] = jnp.concatenate(tiles, axis=0).astype(BF16)

    pl.semaphore_wait(barrier, greeted)

    def remote(src, dst, send, recv, df, ds):
        return pltpu.make_async_remote_copy(
            src_ref=src, dst_ref=dst, send_sem=send, recv_sem=recv,
            device_id=(fi + df, si + ds), device_id_type=MESH)

    def halo_copy(ref, send, recv, ds, f):
        i = (ds > 0) * planes + f
        r0, r1, rn = span(ds, HALO, rows, HALO, tall)
        return remote(ref.at[f, pl.ds(HALO + r1, rn), lanes], ref.at[f, pl.ds(r0, rn), lanes],
                      send.at[i], recv.at[i], 0, ds)

    def sky_copy(ds, f):
        return halo_copy(skyh, s_sky, r_sky, ds, f)

    def gb_copy(ds, f):
        i = (ds > 0) * planes + f
        r0, _, rn = span(ds, HALO, rows, HALO, tall)
        return remote(gs.at[(ds > 0) * 1, f], gbh.at[f, pl.ds(r0, rn), lanes],
                      s_gb.at[i], r_gb.at[i], 0, ds)

    spare = HALO - MAXH
    guest = planes - 1
    assert spare * guest == MAXH
    tile_row = iota((HALO, length), 0)

    def pack_halo(ds, f, own_tile, guest_tile):
        if ds > 0:
            return jnp.where(tile_row < spare,
                             pltpu.roll(guest_tile, HALO - spare * (f + 1), 0), own_tile)
        return jnp.where(tile_row >= MAXH, pltpu.roll(guest_tile, MAXH - spare * f, 0), own_tile)

    def unpack_guest(ds):
        r0, _, rn = span(ds, HALO, rows, HALO, tall)
        tile = jnp.zeros((HALO, length), F32)
        for f in range(guest):
            got = gbh[f, r0:r0 + rn, PAD:PAD + length].astype(F32)
            first = spare * (f + 1) if ds > 0 else spare * f
            shift = first if ds > 0 else (first + HALO - MAXH) % HALO
            here = jnp.logical_and(tile_row >= first, tile_row < first + spare)
            tile = jnp.where(here, pltpu.roll(got, shift, 0) if shift else got, tile)
        gbh[guest, r0:r0 + rn, PAD:PAD + length] = tile.astype(BF16)

    def bm_copy(df):
        j = 0 if df > 0 else 1
        return remote(bm.at[planes if df > 0 else 1], bm.at[0 if df > 0 else planes + 1],
                      s_bm.at[j], r_bm.at[j], df, 0)

    def part_copy(i, df, ds):
        edge = ed if ds > 0 else eu
        if ds == 0:
            src, dst = part.at[planes + 1 if df > 0 else 0], pf.at[0 if df > 0 else 1]
        elif df == 0:
            src, dst = edge.at[pl.ds(1, planes)], pe.at[0 if ds < 0 else 1]
        else:
            src = edge.at[pl.ds(planes + 1 if df > 0 else 0, 1)]
            dst = pc.at[(df > 0) * 2 + (ds > 0)]
        return remote(src, dst, s_part.at[i], r_part.at[i], df, ds)

    own.wait()
    for ds in (-1, 1):
        @pl.when(valid(0, ds))
        def _(ds=ds):
            for f in order:
                sky_copy(ds, f).start()

    def cot_half(g, h):
        return cotv[g, :, h * HALF:(h + 1) * HALF, :].reshape(wide, length)

    def close_plane(p):
        r = iota((HALF, length), 0)
        piece = [acc[p, h, 1] + shift_next(acc[p, h, 0]) + shift_prev(acc[p, h, 2])
                 for h in range(halves)]
        for h in range(halves):
            total = piece[h][:HALF]
            if h > 0:
                total = total + jnp.where(r == 0, piece[h - 1][HALF:HALF + 1], 0.0)
            if h < halves - 1:
                total = total + jnp.where(r == HALF - 1, piece[h + 1][HALF + 1:HALF + 2], 0.0)
            part[p, h * HALF:(h + 1) * HALF] = total
        for ref, line in ((ed, piece[-1][HALF:HALF + 1]), (eu, piece[0][HALF + 1:HALF + 2])):
            n = length // 8
            ref[p] = jnp.concatenate([line[:, j * n:(j + 1) * n] for j in range(8)], axis=0)

    for g in range(planes):
        cot_copies[g].wait()
        for h in range(halves):
            res = jnp.dot(bmat[...], cot_half(g, h), preferred_element_type=F32)
            for a in range(3):
                piece = res[3 * a * EDGE:3 * (a + 1) * EDGE].reshape(3, EDGE, length)
                if g == 0 or a == 2:
                    acc[g + a, h] = piece
                else:
                    acc[g + a, h] += piece
        close_plane(g)
    close_plane(planes)
    close_plane(planes + 1)
    for i, (df, ds) in enumerate(DIRS):
        @pl.when(valid(df, ds))
        def _(i=i, df=df, ds=ds):
            part_copy(i, df, ds).start()

    def make_taps(p):
        h = hwb[p]
        fall = -2.0 / (h * h)

        def profile(d, reach, fall):
            d = d.astype(F32)
            return jnp.where(jnp.abs(d) <= reach, jnp.exp((d * d) * fall), 0.0)

        lane = iota((8, 256), 1)
        small = jnp.where(lane <= 2 * MAXH, profile(lane - MAXH, h, fall), 0.0)
        inv = 1.0 / jnp.sqrt(jnp.sum(small * small, axis=1, keepdims=True))
        inv = jnp.broadcast_to(inv, (8, 256))[0:1]
        h, fall = h[0:1], fall[0:1]
        shape = (3 * BLOCK, BLOCK)
        val = profile(iota(shape, 0) - BLOCK - iota(shape, 1), h[:, :BLOCK], fall[:, :BLOCK]) * inv[:, :BLOCK]
        hi = val.astype(BF16)
        tcol[p, :, 0:BLOCK] = hi
        tcol[p, :, BLOCK:] = (val - hi.astype(F32)).astype(BF16)
        shape = (high, 4 * tall)
        lane = iota(shape, 1)
        row = row_of(lax.rem(iota(shape, 0), EDGE), HALF) + HALF * lax.div(iota(shape, 0), EDGE)
        val = profile(lax.rem(lane, tall) - HALO - row, h, fall) * inv
        hi = val.astype(BF16).astype(F32)
        at = lane - 2 * tall * (order.index(p) % 2)
        here = jnp.logical_and(at >= 0, at < 2 * tall)
        first = jnp.logical_and(at >= 0, at < tall)
        trow[p, 0:high] = jnp.where(here, hi, 0.0).astype(BF16)
        trow[p, high:] = jnp.where(first, val - hi, 0.0).astype(BF16)

    for p in range(planes):
        make_taps(p)

    def blur(src, pair):
        blocks = length // BLOCK
        parts = []
        for p in pair:
            field = jnp.concatenate(
                [src[p, :, j * BLOCK:(j + 3) * BLOCK] for j in range(blocks)], axis=0)
            both = jnp.dot(field, tcol[p], preferred_element_type=F32)
            q = both[:, :BLOCK] + both[:, BLOCK:]
            hi = q.astype(BF16)
            lo = (q - hi.astype(F32)).astype(BF16)
            for x in (hi, lo):
                parts.append(jnp.concatenate(
                    [x[j * tall:(j + 1) * tall] for j in range(blocks)], axis=1))
        left = jnp.concatenate([trow[p] for p in pair], axis=0)
        res = jnp.dot(left, jnp.concatenate(parts, axis=0), preferred_element_type=F32)
        return [res[2 * i * high:(2 * i + 1) * high] + res[(2 * i + 1) * high:(2 * i + 2) * high]
                for i in range(len(pair))]

    def spread_beam(p, beam):
        shifts = (shift_prev(beam), beam, shift_next(beam))
        for h in range(halves):
            bs[h, p] = jnp.concatenate(
                [x[h * EDGE:(h + 1) * EDGE] for x in shifts] + [jnp.zeros((8, length), F32)],
                axis=0).astype(BF16)

    def wait_halos(make, which):
        for ds in (-1, 1):
            @pl.when(valid(0, -ds))
            def _(ds=ds):
                for f in which:
                    make(ds, f).wait_recv()

    def make_beams(pair):
        beams = blur(skyh, pair)
        r = iota(beams[0].shape, 0)
        outside = jnp.logical_or(jnp.logical_and(r == high - EDGE + HALF, si == ns - 1),
                                 jnp.logical_and(r == HALF + 1, si == 0))
        for f, beam in zip(pair, beams):
            beam = jnp.where(outside, 0.0, beam)
            if f in (0, planes - 1):
                bm[f + 1] = beam.astype(BF16)
            spread_beam(f + 1, beam)

    wait_halos(sky_copy, order)
    make_beams(pairs[0])
    for df in (-1, 1):
        @pl.when(valid(df, 0))
        def _(df=df):
            bm_copy(df).start()

    for i, (df, ds) in enumerate(DIRS):
        @pl.when(valid(-df, -ds))
        def _(i=i, df=df, ds=ds):
            part_copy(i, df, ds).wait_recv()
    r = iota((rows, length), 0)
    sums = {}
    for f in order:
        total = part[f + 1]
        if f == 0:
            total = total + pf[0]
        if f == planes - 1:
            total = total + pf[1]
        for up in (0, 1):
            line = pe[up, f]
            if f == 0:
                line = line + pc[2 + up, 0]
            if f == planes - 1:
                line = line + pc[up, 0]
            line = jnp.concatenate([line[k:k + 1] for k in range(8)], axis=1)
            total = total + jnp.where(r == (0 if up else rows - 1), line, 0.0)
        sums[f] = total
        gbh[f, HALO:HALO + rows, PAD:PAD + length] = total.astype(BF16)
    for f in range(guest):
        gs[0, f] = pack_halo(-1, f, sums[f][:HALO], sums[guest][:HALO]).astype(BF16)
        gs[1, f] = pack_halo(1, f, sums[f][rows - HALO:], sums[guest][rows - HALO:]).astype(BF16)
    gb_order = pairs[1] + pairs[0][:1]
    for ds in (-1, 1):
        @pl.when(valid(0, ds))
        def _(ds=ds):
            for f in gb_order:
                gb_copy(ds, f).start()

    for pair in pairs[1:]:
        make_beams(pair)

    acc2 = jnp.zeros((3 * TALL3, wide), F32)
    def gram(total, g):
        for h in range(halves):
            total = total + lax.dot_general(
                bs[h, g:g + 3].reshape(3 * TALL3, length), cot_half(g, h),
                (((1,), (1,)), ((), ())), preferred_element_type=F32)
        return total

    for g in range(1, planes - 1):
        acc2 = gram(acc2, g)
    for df in (-1, 1):
        @pl.when(valid(-df, 0))
        def _(df=df):
            bm_copy(df).wait_recv()
    for p in (0, planes + 1):
        spread_beam(p, bm[p].astype(F32))
    for g in (0, planes - 1):
        acc2 = gram(acc2, g)
    lines = []
    for a in range(3):
        for b in range(3):
            for e in range(3):
                tile = acc2[a * TALL3 + e * EDGE:a * TALL3 + (e + 1) * EDGE]
                lines.append(jnp.sum(jnp.where(masks[b], tile, 0.0), axis=0, keepdims=True))
    lines.append(jnp.zeros((128 - 27, wide), F32))
    terms = lax.dot_general(member.astype(F32), jnp.concatenate(lines, axis=0),
                            (((1,), (1,)), ((), ())), precision=lax.Precision.HIGHEST,
                            preferred_element_type=F32)
    half = chans // 2
    packed = terms[:half] + pltpu.roll(terms[half:], 64, 1)
    mine[...] = packed
    slots[si] = packed

    def kg_copy(k, src, dst, send, recv, at, size, axis):
        to = lax.rem(at + k, size)
        return pltpu.make_async_remote_copy(
            src_ref=src, dst_ref=dst.at[at], send_sem=send.at[k], recv_sem=recv.at[k],
            device_id=(to, si) if axis == 0 else (fi, to), device_id_type=MESH)

    def kg_wait(k, src, dst, send, recv, at, size, axis):
        pltpu.make_async_remote_copy(
            src_ref=src, dst_ref=dst.at[lax.rem(at - k + size, size)], send_sem=send.at[k],
            recv_sem=recv.at[k], device_id=(fi, si), device_id_type=MESH).wait_recv()

    over_sky = (mine, slots, s_kg, r_kg, si, ns, 1)
    over_freq = (mine2, slots2, s_kf, r_kf, fi, nf, 0)
    for k in range(1, ns):
        kg_copy(k, *over_sky).start()

    out_copies = [pltpu.make_async_copy(outv.at[f], out_ref.at[f], out_sem.at[f])
                  for f in range(planes)]

    def finish(pair):
        for f, both in zip(pair, blur(gbh, pair)):
            for h in range(halves):
                outv[f, h * HALF:(h + 1) * HALF] = both[h * EDGE:h * EDGE + HALF]
            out_copies[f].start()

    wait_halos(gb_copy, pairs[1])
    finish(pairs[1])
    for k in range(1, ns):
        kg_wait(k, *over_sky)
    total = slots[0]
    for k in range(1, ns):
        total = total + slots[k]
    mine2[...] = total
    slots2[fi] = total
    for k in range(1, nf):
        kg_copy(k, *over_freq).start()
    wait_halos(gb_copy, pairs[0][:1])
    for ds in (-1, 1):
        unpack_guest(ds)
    finish(pairs[0])
    for k in range(1, nf):
        kg_wait(k, *over_freq)
    total = slots2[0]
    for k in range(1, nf):
        total = total + slots2[k]
    kg_ref[...] = total * scale

    for copy in out_copies:
        copy.wait()
    for i, (df, ds) in enumerate(DIRS):
        @pl.when(valid(df, ds))
        def _(i=i, df=df, ds=ds):
            part_copy(i, df, ds).wait_send()
            if ds == 0:
                bm_copy(df).wait_send()
            if df == 0:
                for f in range(planes):
                    sky_copy(ds, f).wait_send()
                    if f != guest:
                        gb_copy(ds, f).wait_send()
    for k in range(1, ns):
        kg_copy(k, *over_sky).wait_send()
    for k in range(1, nf):
        kg_copy(k, *over_freq).wait_send()


def hand_on(sky_ref, packed_ref, out_ref, kg_ref):
    out_ref[...] = sky_ref[...]

    @pl.when(pl.program_id(0) == 0)
    def _():
        packed = packed_ref[...]
        half = packed.shape[0]
        kg_ref[0:half] = packed[:, :27]
        kg_ref[half:] = pltpu.roll(packed, 64, 1)[:, :27]


def per_device(sky_cube, half_width, conv_weight, out_cotangent):
    planes, rows, length = sky_cube.shape
    chans = conv_weight.shape[0]
    nf, ns = lax.axis_size("freq"), lax.axis_size("sky")
    scale = 1.0 / math.sqrt(planes * nf * rows * ns * length)
    tall = rows + 2 * HALO
    wide = chans * HALF
    halves = rows // HALF
    high = halves * EDGE
    dma = pltpu.SemaphoreType.DMA

    def kernel(*refs):
        body(nf, ns, scale, *refs)

    sky_grad, packed = pl.pallas_call(
        kernel,
        out_shape=(jax.ShapeDtypeStruct((planes, rows, length), F32),
                   jax.ShapeDtypeStruct((chans // 2, 128), F32)),
        in_specs=[pl.BlockSpec(memory_space=pltpu.HBM)] * 4,
        out_specs=(pl.BlockSpec(memory_space=pltpu.HBM), pl.BlockSpec(memory_space=pltpu.VMEM)),
        scratch_shapes=[
            pltpu.VMEM((planes, rows, length), F32), dma((planes,)),
            pltpu.SMEM((planes,), jnp.int32),
            pltpu.VMEM((chans, 27), BF16),
            pltpu.VMEM((planes, tall, length + 2 * PAD), BF16),
            pltpu.VMEM((planes, tall, length + 2 * PAD), BF16),
            pltpu.VMEM((2, planes - 1, HALO, length), BF16),
            pltpu.VMEM((planes, chans, rows, length), BF16),
            pltpu.VMEM((9 * EDGE + 8, wide), BF16),
            pltpu.VMEM((planes + 2, halves, 3, EDGE, length), F32),
            pltpu.VMEM((planes + 2, rows, length), F32),
            pltpu.VMEM((planes + 2, 8, length // 8), F32),
            pltpu.VMEM((planes + 2, 8, length // 8), F32),
            pltpu.VMEM((2, rows, length), F32),
            pltpu.VMEM((2, planes, 8, length // 8), F32),
            pltpu.VMEM((4, 1, 8, length // 8), F32),
            pltpu.VMEM((planes + 2, high, length), BF16),
            pltpu.VMEM((halves, planes + 2, TALL3, length), BF16),
            pltpu.VMEM((planes, 3 * BLOCK, 2 * BLOCK), BF16),
            pltpu.VMEM((planes, 2 * high, 4 * tall), BF16),
            pltpu.VMEM((planes, 8, 256), F32),
            pltpu.VMEM((chans // 2, 128), F32),
            pltpu.VMEM((ns, chans // 2, 128), F32),
            pltpu.VMEM((chans // 2, 128), F32),
            pltpu.VMEM((nf, chans // 2, 128), F32),
            dma((planes,)), dma((3,)),
            dma((2 * planes,)), dma((2 * planes,)), dma((8,)), dma((8,)),
            dma((2 * planes,)), dma((2 * planes,)), dma((2,)), dma((2,)),
            dma((ns,)), dma((ns,)), dma((nf,)), dma((nf,)),
        ],
        compiler_params=pltpu.CompilerParams(
            collective_id=0, has_side_effects=True, vmem_limit_bytes=60 * 1024 * 1024),
        name="beam_backward",
    )(half_width, sky_cube, conv_weight, out_cotangent)
    return pl.pallas_call(
        hand_on,
        out_shape=(jax.ShapeDtypeStruct((planes, rows, length), F32),
                   jax.ShapeDtypeStruct((chans, 27), F32)),
        grid=(2,),
        in_specs=[pl.BlockSpec((planes // 2, rows, length), lambda f: (f, 0, 0)),
                  pl.BlockSpec((chans // 2, 128), lambda f: (0, 0))],
        out_specs=(pl.BlockSpec((planes // 2, rows, length), lambda f: (f, 0, 0)),
                   pl.BlockSpec((chans, 27), lambda f: (0, 0))),
        compiler_params=pltpu.CompilerParams(vmem_limit_bytes=60 * 1024 * 1024),
        name="hand_on",
    )(sky_grad, packed)


def solution(mesh):
    return jax.shard_map(
        per_device,
        mesh=mesh,
        in_specs=(P("freq", "sky", None), P("freq"), P(), P(None, "freq", "sky", None)),
        out_specs=(P("freq", "sky", None), P()),
        check_vma=False,
    )
```

```python
import math

import jax
import jax.numpy as jnp
from jax import lax
from jax.experimental import pallas as pl
from jax.experimental.pallas import tpu as pltpu
from jax.sharding import PartitionSpec as P

MAXH = 12
HALO = 16
PAD = 128
BLOCK = 128
HALF = 16
EDGE = 24
TALL3 = 80
F32 = jnp.float32
BF16 = jnp.bfloat16
MESH = pl.DeviceIdType.MESH
DIRS = [(df, ds) for df in (-1, 0, 1) for ds in (-1, 0, 1) if (df, ds) != (0, 0)]


def iota(shape, dim):
    return lax.broadcasted_iota(jnp.int32, shape, dim)


def row_of(r, rows):
    return jnp.where(r <= rows, r, jnp.where(r == rows + 1, -1, -1000))


def band_mask(b, height, rows, width):
    shape = (height, width)
    return row_of(iota(shape, 0), rows) == lax.rem(iota(shape, 1), rows) + (b - 1)


def shift_next(x):
    n = x.shape[-1]
    return jnp.where(iota(x.shape, 1) == n - 1, 0.0, pltpu.roll(x, n - 1, 1))


def shift_prev(x):
    n = x.shape[-1]
    return jnp.where(iota(x.shape, 1) == 0, 0.0, pltpu.roll(x, 1, 1))


def body(nf, ns, scale, hw_hbm, sky_ref, w_hbm, cot_ref, out_ref, kg_ref,
         outv, out_sem, hw_ref, w_ref, skyh, gbh, cotv, bmat, acc, part, eu, ed, pf, pe, pc,
         bm, bs, tcol, trow, hwb, mine, slots, mine2, slots2,
         cot_sem, own_sem, s_sky, r_sky, s_part, r_part, s_gb, r_gb, s_bm, r_bm,
         s_kg, r_kg, s_kf, r_kf):
    planes, rows, length = out_ref.shape
    chans = w_ref.shape[0]
    wide = chans * HALF
    halves = rows // HALF
    high = halves * EDGE
    tall = rows + 2 * HALO
    fi, si = lax.axis_index("freq"), lax.axis_index("sky")

    def valid(df, ds):
        ok = None
        for at, step, size in ((fi, df, nf), (si, ds, ns)):
            if step:
                one = at + step < size if step > 0 else at + step >= 0
                ok = one if ok is None else jnp.logical_and(ok, one)
        return ok

    def span(step, own_lo, own_n, halo_n, full_n):
        if step == 0:
            return own_lo, 0, own_n
        if step > 0:
            return own_lo - halo_n, own_n - halo_n, halo_n
        return own_lo + own_n, 0, halo_n

    lanes = pl.ds(PAD, length)
    order = [0, planes - 1] + list(range(1, planes - 1))
    pairs = [order[k:k + 2] for k in range(0, planes, 2)]

    own_w = pltpu.make_async_copy(w_hbm, w_ref, own_sem.at[1])
    own_w.start()
    own_hw = pltpu.make_async_copy(hw_hbm, hw_ref, own_sem.at[2])
    own_hw.start()
    cot_copies = [pltpu.make_async_copy(cot_ref.at[:, g], cotv.at[g], cot_sem.at[g])
                  for g in range(planes)]
    for copy in cot_copies:
        copy.start()
    own = pltpu.make_async_copy(
        sky_ref, skyh.at[:, pl.ds(HALO, rows), lanes], own_sem.at[0])
    own.start()

    for df, ds in DIRS:
        @pl.when(jnp.logical_not(valid(-df, -ds)))
        def _(df=df, ds=ds):
            if df == 0:
                r0, _, rn = span(ds, HALO, rows, HALO, tall)
                zero = jnp.zeros((planes, rn, length), BF16)
                skyh[:, r0:r0 + rn, PAD:PAD + length] = zero
                gbh[:, r0:r0 + rn, PAD:PAD + length] = zero
                pe[0 if ds < 0 else 1] = jnp.zeros((planes, 8, length // 8), F32)
            elif ds == 0:
                bm[0 if df > 0 else planes + 1] = jnp.zeros((high, length), BF16)
                pf[0 if df > 0 else 1] = jnp.zeros((rows, length), F32)
            else:
                pc[(df > 0) * 2 + (ds > 0)] = jnp.zeros((1, 8, length // 8), F32)

    barrier = pltpu.get_barrier_semaphore()
    for k in range(1, ns):
        pl.semaphore_signal(barrier, inc=1, device_id=(fi, lax.rem(si + k, ns)), device_id_type=MESH)
    for k in range(1, nf):
        pl.semaphore_signal(barrier, inc=1, device_id=(lax.rem(fi + k, nf), si), device_id_type=MESH)
    greeted = jnp.int32(ns + nf - 2)
    for df, ds in DIRS:
        if df and ds:
            ok = valid(df, ds)
            greeted = greeted + jnp.where(ok, 1, 0)

            @pl.when(ok)
            def _(df=df, ds=ds):
                pl.semaphore_signal(barrier, inc=1, device_id=(fi + df, si + ds), device_id_type=MESH)

    for ref in (skyh, gbh):
        n = ref.shape[0]
        ref[:, :, 0:PAD] = jnp.zeros((n, tall, PAD), BF16)
        ref[:, :, PAD + length:] = jnp.zeros((n, tall, PAD), BF16)
    own_hw.wait()
    for k in range(planes):
        hwb[k] = jnp.full((8, 256), hw_ref[k].astype(F32))
    own_w.wait()
    member = (lax.div(iota((chans, wide), 1), HALF) == iota((chans, wide), 0))
    spread = lax.dot_general(w_ref[...], member.astype(BF16), (((0,), (0,)), ((), ())),
                             preferred_element_type=F32)
    masks = [band_mask(b, EDGE, HALF, wide) for b in range(3)]
    tiles = []
    for a in range(3):
        for e in range(3):
            tile = jnp.zeros((EDGE, wide), F32)
            for b in range(3):
                k = 9 * a + 3 * b + e
                tile = tile + jnp.where(masks[b], spread[k:k + 1, :], 0.0)
            tiles.append(tile)
    tiles.append(jnp.zeros((8, wide), F32))
    bmat[...] = jnp.concatenate(tiles, axis=0).astype(BF16)

    pl.semaphore_wait(barrier, greeted)

    def remote(src, dst, send, recv, df, ds):
        return pltpu.make_async_remote_copy(
            src_ref=src, dst_ref=dst, send_sem=send, recv_sem=recv,
            device_id=(fi + df, si + ds), device_id_type=MESH)

    def halo_copy(ref, send, recv, ds, f):
        i = (ds > 0) * planes + f
        r0, r1, rn = span(ds, HALO, rows, HALO, tall)
        return remote(ref.at[f, pl.ds(HALO + r1, rn), lanes], ref.at[f, pl.ds(r0, rn), lanes],
                      send.at[i], recv.at[i], 0, ds)

    def sky_copy(ds, f):
        return halo_copy(skyh, s_sky, r_sky, ds, f)

    def gb_copy(ds, f):
        return halo_copy(gbh, s_gb, r_gb, ds, f)

    def bm_copy(df):
        j = 0 if df > 0 else 1
        return remote(bm.at[planes if df > 0 else 1], bm.at[0 if df > 0 else planes + 1],
                      s_bm.at[j], r_bm.at[j], df, 0)

    def part_copy(i, df, ds):
        edge = ed if ds > 0 else eu
        if ds == 0:
            src, dst = part.at[planes + 1 if df > 0 else 0], pf.at[0 if df > 0 else 1]
        elif df == 0:
            src, dst = edge.at[pl.ds(1, planes)], pe.at[0 if ds < 0 else 1]
        else:
            src = edge.at[pl.ds(planes + 1 if df > 0 else 0, 1)]
            dst = pc.at[(df > 0) * 2 + (ds > 0)]
        return remote(src, dst, s_part.at[i], r_part.at[i], df, ds)

    own.wait()
    for ds in (-1, 1):
        @pl.when(valid(0, ds))
        def _(ds=ds):
            for f in order:
                sky_copy(ds, f).start()

    def cot_half(g, h):
        return cotv[g, :, h * HALF:(h + 1) * HALF, :].reshape(wide, length)

    def close_plane(p):
        r = iota((HALF, length), 0)
        piece = [acc[p, h, 1] + shift_next(acc[p, h, 0]) + shift_prev(acc[p, h, 2])
                 for h in range(halves)]
        for h in range(halves):
            total = piece[h][:HALF]
            if h > 0:
                total = total + jnp.where(r == 0, piece[h - 1][HALF:HALF + 1], 0.0)
            if h < halves - 1:
                total = total + jnp.where(r == HALF - 1, piece[h + 1][HALF + 1:HALF + 2], 0.0)
            part[p, h * HALF:(h + 1) * HALF] = total
        for ref, line in ((ed, piece[-1][HALF:HALF + 1]), (eu, piece[0][HALF + 1:HALF + 2])):
            n = length // 8
            ref[p] = jnp.concatenate([line[:, j * n:(j + 1) * n] for j in range(8)], axis=0)

    for g in range(planes):
        cot_copies[g].wait()
        for h in range(halves):
            res = jnp.dot(bmat[...], cot_half(g, h), preferred_element_type=F32)
            for a in range(3):
                piece = res[3 * a * EDGE:3 * (a + 1) * EDGE].reshape(3, EDGE, length)
                if g == 0 or a == 2:
                    acc[g + a, h] = piece
                else:
                    acc[g + a, h] += piece
        close_plane(g)
    close_plane(planes)
    close_plane(planes + 1)
    for i, (df, ds) in enumerate(DIRS):
        @pl.when(valid(df, ds))
        def _(i=i, df=df, ds=ds):
            part_copy(i, df, ds).start()

    def make_taps(p):
        h = hwb[p]
        fall = -2.0 / (h * h)

        def profile(d, reach, fall):
            d = d.astype(F32)
            return jnp.where(jnp.abs(d) <= reach, jnp.exp((d * d) * fall), 0.0)

        lane = iota((8, 256), 1)
        small = jnp.where(lane <= 2 * MAXH, profile(lane - MAXH, h, fall), 0.0)
        inv = 1.0 / jnp.sqrt(jnp.sum(small * small, axis=1, keepdims=True))
        inv = jnp.broadcast_to(inv, (8, 256))[0:1]
        h, fall = h[0:1], fall[0:1]
        shape = (3 * BLOCK, BLOCK)
        val = profile(iota(shape, 0) - BLOCK - iota(shape, 1), h[:, :BLOCK], fall[:, :BLOCK]) * inv[:, :BLOCK]
        hi = val.astype(BF16)
        tcol[p, :, 0:BLOCK] = hi
        tcol[p, :, BLOCK:] = (val - hi.astype(F32)).astype(BF16)
        shape = (high, 4 * tall)
        lane = iota(shape, 1)
        row = row_of(lax.rem(iota(shape, 0), EDGE), HALF) + HALF * lax.div(iota(shape, 0), EDGE)
        val = profile(lax.rem(lane, tall) - HALO - row, h, fall) * inv
        hi = val.astype(BF16).astype(F32)
        at = lane - 2 * tall * (order.index(p) % 2)
        here = jnp.logical_and(at >= 0, at < 2 * tall)
        first = jnp.logical_and(at >= 0, at < tall)
        trow[p, 0:high] = jnp.where(here, hi, 0.0).astype(BF16)
        trow[p, high:] = jnp.where(first, val - hi, 0.0).astype(BF16)

    for p in range(planes):
        make_taps(p)

    def blur(src, pair):
        blocks = length // BLOCK
        parts = []
        for p in pair:
            field = jnp.concatenate(
                [src[p, :, j * BLOCK:(j + 3) * BLOCK] for j in range(blocks)], axis=0)
            both = jnp.dot(field, tcol[p], preferred_element_type=F32)
            q = both[:, :BLOCK] + both[:, BLOCK:]
            hi = q.astype(BF16)
            lo = (q - hi.astype(F32)).astype(BF16)
            for x in (hi, lo):
                parts.append(jnp.concatenate(
                    [x[j * tall:(j + 1) * tall] for j in range(blocks)], axis=1))
        left = jnp.concatenate([trow[p] for p in pair], axis=0)
        res = jnp.dot(left, jnp.concatenate(parts, axis=0), preferred_element_type=F32)
        return [res[2 * i * high:(2 * i + 1) * high] + res[(2 * i + 1) * high:(2 * i + 2) * high]
                for i in range(len(pair))]

    def spread_beam(p, beam):
        shifts = (shift_prev(beam), beam, shift_next(beam))
        for h in range(halves):
            bs[h, p] = jnp.concatenate(
                [x[h * EDGE:(h + 1) * EDGE] for x in shifts] + [jnp.zeros((8, length), F32)],
                axis=0).astype(BF16)

    def wait_halos(make, which):
        for ds in (-1, 1):
            @pl.when(valid(0, -ds))
            def _(ds=ds):
                for f in which:
                    make(ds, f).wait_recv()

    def make_beams(pair):
        beams = blur(skyh, pair)
        r = iota(beams[0].shape, 0)
        outside = jnp.logical_or(jnp.logical_and(r == high - EDGE + HALF, si == ns - 1),
                                 jnp.logical_and(r == HALF + 1, si == 0))
        for f, beam in zip(pair, beams):
            beam = jnp.where(outside, 0.0, beam)
            if f in (0, planes - 1):
                bm[f + 1] = beam.astype(BF16)
            spread_beam(f + 1, beam)

    wait_halos(sky_copy, order)
    make_beams(pairs[0])
    for df in (-1, 1):
        @pl.when(valid(df, 0))
        def _(df=df):
            bm_copy(df).start()

    for i, (df, ds) in enumerate(DIRS):
        @pl.when(valid(-df, -ds))
        def _(i=i, df=df, ds=ds):
            part_copy(i, df, ds).wait_recv()
    r = iota((rows, length), 0)
    for f in order:
        total = part[f + 1]
        if f == 0:
            total = total + pf[0]
        if f == planes - 1:
            total = total + pf[1]
        for up in (0, 1):
            line = pe[up, f]
            if f == 0:
                line = line + pc[2 + up, 0]
            if f == planes - 1:
                line = line + pc[up, 0]
            line = jnp.concatenate([line[k:k + 1] for k in range(8)], axis=1)
            total = total + jnp.where(r == (0 if up else rows - 1), line, 0.0)
        gbh[f, HALO:HALO + rows, PAD:PAD + length] = total.astype(BF16)
    for ds in (-1, 1):
        @pl.when(valid(0, ds))
        def _(ds=ds):
            for f in order:
                gb_copy(ds, f).start()

    for pair in pairs[1:]:
        make_beams(pair)

    acc2 = jnp.zeros((3 * TALL3, wide), F32)
    def gram(total, g):
        for h in range(halves):
            total = total + lax.dot_general(
                bs[h, g:g + 3].reshape(3 * TALL3, length), cot_half(g, h),
                (((1,), (1,)), ((), ())), preferred_element_type=F32)
        return total

    for g in range(1, planes - 1):
        acc2 = gram(acc2, g)
    for df in (-1, 1):
        @pl.when(valid(-df, 0))
        def _(df=df):
            bm_copy(df).wait_recv()
    for p in (0, planes + 1):
        spread_beam(p, bm[p].astype(F32))
    for g in (0, planes - 1):
        acc2 = gram(acc2, g)
    lines = []
    for a in range(3):
        for b in range(3):
            for e in range(3):
                tile = acc2[a * TALL3 + e * EDGE:a * TALL3 + (e + 1) * EDGE]
                lines.append(jnp.sum(jnp.where(masks[b], tile, 0.0), axis=0, keepdims=True))
    lines.append(jnp.zeros((128 - 27, wide), F32))
    terms = lax.dot_general(member.astype(F32), jnp.concatenate(lines, axis=0),
                            (((1,), (1,)), ((), ())), precision=lax.Precision.HIGHEST,
                            preferred_element_type=F32)
    half = chans // 2
    packed = terms[:half] + pltpu.roll(terms[half:], 64, 1)
    mine[...] = packed
    slots[si] = packed

    def kg_copy(k, src, dst, send, recv, at, size, axis):
        to = lax.rem(at + k, size)
        return pltpu.make_async_remote_copy(
            src_ref=src, dst_ref=dst.at[at], send_sem=send.at[k], recv_sem=recv.at[k],
            device_id=(to, si) if axis == 0 else (fi, to), device_id_type=MESH)

    def kg_wait(k, src, dst, send, recv, at, size, axis):
        pltpu.make_async_remote_copy(
            src_ref=src, dst_ref=dst.at[lax.rem(at - k + size, size)], send_sem=send.at[k],
            recv_sem=recv.at[k], device_id=(fi, si), device_id_type=MESH).wait_recv()

    over_sky = (mine, slots, s_kg, r_kg, si, ns, 1)
    over_freq = (mine2, slots2, s_kf, r_kf, fi, nf, 0)
    for k in range(1, ns):
        kg_copy(k, *over_sky).start()

    out_copies = [pltpu.make_async_copy(outv.at[f], out_ref.at[f], out_sem.at[f])
                  for f in range(planes)]

    def finish(pair):
        for f, both in zip(pair, blur(gbh, pair)):
            for h in range(halves):
                outv[f, h * HALF:(h + 1) * HALF] = both[h * EDGE:h * EDGE + HALF]
            out_copies[f].start()

    wait_halos(gb_copy, order)
    finish(pairs[0])
    for k in range(1, ns):
        kg_wait(k, *over_sky)
    total = slots[0]
    for k in range(1, ns):
        total = total + slots[k]
    mine2[...] = total
    slots2[fi] = total
    for k in range(1, nf):
        kg_copy(k, *over_freq).start()
    for pair in pairs[1:]:
        finish(pair)
    for k in range(1, nf):
        kg_wait(k, *over_freq)
    total = slots2[0]
    for k in range(1, nf):
        total = total + slots2[k]
    kg_ref[...] = total * scale

    for copy in out_copies:
        copy.wait()
    for i, (df, ds) in enumerate(DIRS):
        @pl.when(valid(df, ds))
        def _(i=i, df=df, ds=ds):
            part_copy(i, df, ds).wait_send()
            if ds == 0:
                bm_copy(df).wait_send()
            if df == 0:
                for f in range(planes):
                    sky_copy(ds, f).wait_send()
                    gb_copy(ds, f).wait_send()
    for k in range(1, ns):
        kg_copy(k, *over_sky).wait_send()
    for k in range(1, nf):
        kg_copy(k, *over_freq).wait_send()


def hand_on(sky_ref, packed_ref, out_ref, kg_ref, held, in_sem, out_sem):
    planes = sky_ref.shape[0]
    arrive = [pltpu.make_async_copy(sky_ref.at[f], held.at[f], in_sem.at[f]) for f in range(planes)]
    leave = [pltpu.make_async_copy(held.at[f], out_ref.at[f], out_sem.at[f]) for f in range(planes)]
    for copy in arrive:
        copy.start()
    for f in range(planes):
        arrive[f].wait()
        leave[f].start()
    packed = packed_ref[...]
    half = packed.shape[0]
    kg_ref[0:half] = packed[:, :27]
    kg_ref[half:] = pltpu.roll(packed, 64, 1)[:, :27]
    for copy in leave:
        copy.wait()


def per_device(sky_cube, half_width, conv_weight, out_cotangent):
    planes, rows, length = sky_cube.shape
    chans = conv_weight.shape[0]
    nf, ns = lax.axis_size("freq"), lax.axis_size("sky")
    scale = 1.0 / math.sqrt(planes * nf * rows * ns * length)
    tall = rows + 2 * HALO
    wide = chans * HALF
    halves = rows // HALF
    high = halves * EDGE
    dma = pltpu.SemaphoreType.DMA

    def kernel(*refs):
        body(nf, ns, scale, *refs)

    sky_grad, packed = pl.pallas_call(
        kernel,
        out_shape=(jax.ShapeDtypeStruct((planes, rows, length), F32),
                   jax.ShapeDtypeStruct((chans // 2, 128), F32)),
        in_specs=[pl.BlockSpec(memory_space=pltpu.HBM)] * 4,
        out_specs=(pl.BlockSpec(memory_space=pltpu.HBM), pl.BlockSpec(memory_space=pltpu.VMEM)),
        scratch_shapes=[
            pltpu.VMEM((planes, rows, length), F32), dma((planes,)),
            pltpu.SMEM((planes,), jnp.int32),
            pltpu.VMEM((chans, 27), BF16),
            pltpu.VMEM((planes, tall, length + 2 * PAD), BF16),
            pltpu.VMEM((planes, tall, length + 2 * PAD), BF16),
            pltpu.VMEM((planes, chans, rows, length), BF16),
            pltpu.VMEM((9 * EDGE + 8, wide), BF16),
            pltpu.VMEM((planes + 2, halves, 3, EDGE, length), F32),
            pltpu.VMEM((planes + 2, rows, length), F32),
            pltpu.VMEM((planes + 2, 8, length // 8), F32),
            pltpu.VMEM((planes + 2, 8, length // 8), F32),
            pltpu.VMEM((2, rows, length), F32),
            pltpu.VMEM((2, planes, 8, length // 8), F32),
            pltpu.VMEM((4, 1, 8, length // 8), F32),
            pltpu.VMEM((planes + 2, high, length), BF16),
            pltpu.VMEM((halves, planes + 2, TALL3, length), BF16),
            pltpu.VMEM((planes, 3 * BLOCK, 2 * BLOCK), BF16),
            pltpu.VMEM((planes, 2 * high, 4 * tall), BF16),
            pltpu.VMEM((planes, 8, 256), F32),
            pltpu.VMEM((chans // 2, 128), F32),
            pltpu.VMEM((ns, chans // 2, 128), F32),
            pltpu.VMEM((chans // 2, 128), F32),
            pltpu.VMEM((nf, chans // 2, 128), F32),
            dma((planes,)), dma((3,)),
            dma((2 * planes,)), dma((2 * planes,)), dma((8,)), dma((8,)),
            dma((2 * planes,)), dma((2 * planes,)), dma((2,)), dma((2,)),
            dma((ns,)), dma((ns,)), dma((nf,)), dma((nf,)),
        ],
        compiler_params=pltpu.CompilerParams(
            collective_id=0, has_side_effects=True, vmem_limit_bytes=60 * 1024 * 1024),
        name="beam_backward",
    )(half_width, sky_cube, conv_weight, out_cotangent)
    return pl.pallas_call(
        hand_on,
        out_shape=(jax.ShapeDtypeStruct((planes, rows, length), F32),
                   jax.ShapeDtypeStruct((chans, 27), F32)),
        in_specs=[pl.BlockSpec(memory_space=pltpu.HBM), pl.BlockSpec(memory_space=pltpu.VMEM)],
        out_specs=(pl.BlockSpec(memory_space=pltpu.HBM), pl.BlockSpec(memory_space=pltpu.VMEM)),
        scratch_shapes=[pltpu.VMEM((planes, rows, length), F32), dma((planes,)), dma((planes,))],
        compiler_params=pltpu.CompilerParams(vmem_limit_bytes=60 * 1024 * 1024),
        name="hand_on",
    )(sky_grad, packed)


def solution(mesh):
    return jax.shard_map(
        per_device,
        mesh=mesh,
        in_specs=(P("freq", "sky", None), P("freq"), P(), P(None, "freq", "sky", None)),
        out_specs=(P("freq", "sky", None), P()),
        check_vma=False,
    )
```

```python
import math

import jax
import jax.numpy as jnp
from jax import lax
from jax.experimental import pallas as pl
from jax.experimental.pallas import tpu as pltpu
from jax.sharding import PartitionSpec as P

MAXH = 12
HALO = 16
PAD = 128
BLOCK = 128
HALF = 16
EDGE = 24
TALL3 = 80
F32 = jnp.float32
BF16 = jnp.bfloat16
MESH = pl.DeviceIdType.MESH
DIRS = [(df, ds) for df in (-1, 0, 1) for ds in (-1, 0, 1) if (df, ds) != (0, 0)]


def iota(shape, dim):
    return lax.broadcasted_iota(jnp.int32, shape, dim)


def row_of(r, rows):
    return jnp.where(r <= rows, r, jnp.where(r == rows + 1, -1, -1000))


def band_mask(b, height, rows, width):
    shape = (height, width)
    return row_of(iota(shape, 0), rows) == lax.rem(iota(shape, 1), rows) + (b - 1)


def shift_next(x):
    n = x.shape[-1]
    return jnp.where(iota(x.shape, 1) == n - 1, 0.0, pltpu.roll(x, n - 1, 1))


def shift_prev(x):
    n = x.shape[-1]
    return jnp.where(iota(x.shape, 1) == 0, 0.0, pltpu.roll(x, 1, 1))


def body(nf, ns, scale, hw_hbm, sky_ref, w_hbm, cot_ref, out_ref, kg_ref,
         outv, out_sem, hw_ref, w_ref, skyh, gbh, cotv, bmat, acc, part, eu, ed, pf, pe, pc,
         bm, bs, tcol, trow, hwb, mine, slots, mine2, slots2,
         cot_sem, own_sem, s_sky, r_sky, s_part, r_part, s_gb, r_gb, s_bm, r_bm,
         s_kg, r_kg, s_kf, r_kf):
    planes, rows, length = out_ref.shape
    chans = w_ref.shape[0]
    wide = chans * HALF
    halves = rows // HALF
    high = halves * EDGE
    tall = rows + 2 * HALO
    fi, si = lax.axis_index("freq"), lax.axis_index("sky")

    def valid(df, ds):
        ok = None
        for at, step, size in ((fi, df, nf), (si, ds, ns)):
            if step:
                one = at + step < size if step > 0 else at + step >= 0
                ok = one if ok is None else jnp.logical_and(ok, one)
        return ok

    def span(step, own_lo, own_n, halo_n, full_n):
        if step == 0:
            return own_lo, 0, own_n
        if step > 0:
            return own_lo - halo_n, own_n - halo_n, halo_n
        return own_lo + own_n, 0, halo_n

    lanes = pl.ds(PAD, length)
    order = [0, planes - 1] + list(range(1, planes - 1))
    pairs = [order[k:k + 2] for k in range(0, planes, 2)]

    own_w = pltpu.make_async_copy(w_hbm, w_ref, own_sem.at[1])
    own_w.start()
    own_hw = pltpu.make_async_copy(hw_hbm, hw_ref, own_sem.at[2])
    own_hw.start()
    cot_copies = [pltpu.make_async_copy(cot_ref.at[:, g], cotv.at[g], cot_sem.at[g])
                  for g in range(planes)]
    for copy in cot_copies:
        copy.start()
    own = pltpu.make_async_copy(
        sky_ref, skyh.at[:, pl.ds(HALO, rows), lanes], own_sem.at[0])
    own.start()

    for df, ds in DIRS:
        @pl.when(jnp.logical_not(valid(-df, -ds)))
        def _(df=df, ds=ds):
            if df == 0:
                r0, _, rn = span(ds, HALO, rows, HALO, tall)
                zero = jnp.zeros((planes, rn, length), BF16)
                skyh[:, r0:r0 + rn, PAD:PAD + length] = zero
                gbh[:, r0:r0 + rn, PAD:PAD + length] = zero
                pe[0 if ds < 0 else 1] = jnp.zeros((planes, 8, length // 8), F32)
            elif ds == 0:
                bm[0 if df > 0 else planes + 1] = jnp.zeros((high, length), BF16)
                pf[0 if df > 0 else 1] = jnp.zeros((rows, length), F32)
            else:
                pc[(df > 0) * 2 + (ds > 0)] = jnp.zeros((1, 8, length // 8), F32)

    barrier = pltpu.get_barrier_semaphore()
    for k in range(1, ns):
        pl.semaphore_signal(barrier, inc=1, device_id=(fi, lax.rem(si + k, ns)), device_id_type=MESH)
    for k in range(1, nf):
        pl.semaphore_signal(barrier, inc=1, device_id=(lax.rem(fi + k, nf), si), device_id_type=MESH)
    greeted = jnp.int32(ns + nf - 2)
    for df, ds in DIRS:
        if df and ds:
            ok = valid(df, ds)
            greeted = greeted + jnp.where(ok, 1, 0)

            @pl.when(ok)
            def _(df=df, ds=ds):
                pl.semaphore_signal(barrier, inc=1, device_id=(fi + df, si + ds), device_id_type=MESH)

    for ref in (skyh, gbh):
        n = ref.shape[0]
        ref[:, :, 0:PAD] = jnp.zeros((n, tall, PAD), BF16)
        ref[:, :, PAD + length:] = jnp.zeros((n, tall, PAD), BF16)
    own_hw.wait()
    for k in range(planes):
        hwb[k] = jnp.full((8, 256), hw_ref[k].astype(F32))
    own_w.wait()
    member = (lax.div(iota((chans, wide), 1), HALF) == iota((chans, wide), 0))
    spread = lax.dot_general(w_ref[...], member.astype(BF16), (((0,), (0,)), ((), ())),
                             preferred_element_type=F32)
    masks = [band_mask(b, EDGE, HALF, wide) for b in range(3)]
    tiles = []
    for a in range(3):
        for e in range(3):
            tile = jnp.zeros((EDGE, wide), F32)
            for b in range(3):
                k = 9 * a + 3 * b + e
                tile = tile + jnp.where(masks[b], spread[k:k + 1, :], 0.0)
            tiles.append(tile)
    tiles.append(jnp.zeros((8, wide), F32))
    bmat[...] = jnp.concatenate(tiles, axis=0).astype(BF16)

    pl.semaphore_wait(barrier, greeted)

    def remote(src, dst, send, recv, df, ds):
        return pltpu.make_async_remote_copy(
            src_ref=src, dst_ref=dst, send_sem=send, recv_sem=recv,
            device_id=(fi + df, si + ds), device_id_type=MESH)

    def halo_copy(ref, send, recv, ds, f):
        i = (ds > 0) * planes + f
        r0, r1, rn = span(ds, HALO, rows, HALO, tall)
        return remote(ref.at[f, pl.ds(HALO + r1, rn), lanes], ref.at[f, pl.ds(r0, rn), lanes],
                      send.at[i], recv.at[i], 0, ds)

    def sky_copy(ds, f):
        return halo_copy(skyh, s_sky, r_sky, ds, f)

    def gb_copy(ds, f):
        return halo_copy(gbh, s_gb, r_gb, ds, f)

    def bm_copy(df):
        j = 0 if df > 0 else 1
        return remote(bm.at[planes if df > 0 else 1], bm.at[0 if df > 0 else planes + 1],
                      s_bm.at[j], r_bm.at[j], df, 0)

    def part_copy(i, df, ds):
        edge = ed if ds > 0 else eu
        if ds == 0:
            src, dst = part.at[planes + 1 if df > 0 else 0], pf.at[0 if df > 0 else 1]
        elif df == 0:
            src, dst = edge.at[pl.ds(1, planes)], pe.at[0 if ds < 0 else 1]
        else:
            src = edge.at[pl.ds(planes + 1 if df > 0 else 0, 1)]
            dst = pc.at[(df > 0) * 2 + (ds > 0)]
        return remote(src, dst, s_part.at[i], r_part.at[i], df, ds)

    own.wait()
    for ds in (-1, 1):
        @pl.when(valid(0, ds))
        def _(ds=ds):
            for f in order:
                sky_copy(ds, f).start()

    def cot_half(g, h):
        return cotv[g, :, h * HALF:(h + 1) * HALF, :].reshape(wide, length)

    def close_plane(p):
        r = iota((HALF, length), 0)
        piece = [acc[p, h, 1] + shift_next(acc[p, h, 0]) + shift_prev(acc[p, h, 2])
                 for h in range(halves)]
        for h in range(halves):
            total = piece[h][:HALF]
            if h > 0:
                total = total + jnp.where(r == 0, piece[h - 1][HALF:HALF + 1], 0.0)
            if h < halves - 1:
                total = total + jnp.where(r == HALF - 1, piece[h + 1][HALF + 1:HALF + 2], 0.0)
            part[p, h * HALF:(h + 1) * HALF] = total
        for ref, line in ((ed, piece[-1][HALF:HALF + 1]), (eu, piece[0][HALF + 1:HALF + 2])):
            n = length // 8
            ref[p] = jnp.concatenate([line[:, j * n:(j + 1) * n] for j in range(8)], axis=0)

    for g in range(planes):
        cot_copies[g].wait()
        for h in range(halves):
            res = jnp.dot(bmat[...], cot_half(g, h), preferred_element_type=F32)
            for a in range(3):
                piece = res[3 * a * EDGE:3 * (a + 1) * EDGE].reshape(3, EDGE, length)
                if g == 0 or a == 2:
                    acc[g + a, h] = piece
                else:
                    acc[g + a, h] += piece
        close_plane(g)
    close_plane(planes)
    close_plane(planes + 1)
    for i, (df, ds) in enumerate(DIRS):
        @pl.when(valid(df, ds))
        def _(i=i, df=df, ds=ds):
            part_copy(i, df, ds).start()

    def make_taps(p):
        h = hwb[p]
        fall = -2.0 / (h * h)

        def profile(d, reach, fall):
            d = d.astype(F32)
            return jnp.where(jnp.abs(d) <= reach, jnp.exp((d * d) * fall), 0.0)

        lane = iota((8, 256), 1)
        small = jnp.where(lane <= 2 * MAXH, profile(lane - MAXH, h, fall), 0.0)
        inv = 1.0 / jnp.sqrt(jnp.sum(small * small, axis=1, keepdims=True))
        inv = jnp.broadcast_to(inv, (8, 256))[0:1]
        h, fall = h[0:1], fall[0:1]
        shape = (3 * BLOCK, BLOCK)
        val = profile(iota(shape, 0) - BLOCK - iota(shape, 1), h[:, :BLOCK], fall[:, :BLOCK]) * inv[:, :BLOCK]
        hi = val.astype(BF16)
        tcol[p, :, 0:BLOCK] = hi
        tcol[p, :, BLOCK:] = (val - hi.astype(F32)).astype(BF16)
        shape = (high, 4 * tall)
        lane = iota(shape, 1)
        row = row_of(lax.rem(iota(shape, 0), EDGE), HALF) + HALF * lax.div(iota(shape, 0), EDGE)
        val = profile(lax.rem(lane, tall) - HALO - row, h, fall) * inv
        hi = val.astype(BF16).astype(F32)
        at = lane - 2 * tall * (order.index(p) % 2)
        here = jnp.logical_and(at >= 0, at < 2 * tall)
        first = jnp.logical_and(at >= 0, at < tall)
        trow[p, 0:high] = jnp.where(here, hi, 0.0).astype(BF16)
        trow[p, high:] = jnp.where(first, val - hi, 0.0).astype(BF16)

    for p in range(planes):
        make_taps(p)

    def blur(src, pair):
        blocks = length // BLOCK
        parts = []
        for p in pair:
            field = jnp.concatenate(
                [src[p, :, j * BLOCK:(j + 3) * BLOCK] for j in range(blocks)], axis=0)
            both = jnp.dot(field, tcol[p], preferred_element_type=F32)
            q = both[:, :BLOCK] + both[:, BLOCK:]
            hi = q.astype(BF16)
            lo = (q - hi.astype(F32)).astype(BF16)
            for x in (hi, lo):
                parts.append(jnp.concatenate(
                    [x[j * tall:(j + 1) * tall] for j in range(blocks)], axis=1))
        left = jnp.concatenate([trow[p] for p in pair], axis=0)
        res = jnp.dot(left, jnp.concatenate(parts, axis=0), preferred_element_type=F32)
        return [res[2 * i * high:(2 * i + 1) * high] + res[(2 * i + 1) * high:(2 * i + 2) * high]
                for i in range(len(pair))]

    def spread_beam(p, beam):
        shifts = (shift_prev(beam), beam, shift_next(beam))
        for h in range(halves):
            bs[h, p] = jnp.concatenate(
                [x[h * EDGE:(h + 1) * EDGE] for x in shifts] + [jnp.zeros((8, length), F32)],
                axis=0).astype(BF16)

    def wait_halos(make, which):
        for ds in (-1, 1):
            @pl.when(valid(0, -ds))
            def _(ds=ds):
                for f in which:
                    make(ds, f).wait_recv()

    def make_beams(pair):
        beams = blur(skyh, pair)
        r = iota(beams[0].shape, 0)
        outside = jnp.logical_or(jnp.logical_and(r == high - EDGE + HALF, si == ns - 1),
                                 jnp.logical_and(r == HALF + 1, si == 0))
        for f, beam in zip(pair, beams):
            beam = jnp.where(outside, 0.0, beam)
            if f in (0, planes - 1):
                bm[f + 1] = beam.astype(BF16)
            spread_beam(f + 1, beam)

    wait_halos(sky_copy, order)
    make_beams(pairs[0])
    for df in (-1, 1):
        @pl.when(valid(df, 0))
        def _(df=df):
            bm_copy(df).start()

    for i, (df, ds) in enumerate(DIRS):
        @pl.when(valid(-df, -ds))
        def _(i=i, df=df, ds=ds):
            part_copy(i, df, ds).wait_recv()
    r = iota((rows, length), 0)
    for f in order:
        total = part[f + 1]
        if f == 0:
            total = total + pf[0]
        if f == planes - 1:
            total = total + pf[1]
        for up in (0, 1):
            line = pe[up, f]
            if f == 0:
                line = line + pc[2 + up, 0]
            if f == planes - 1:
                line = line + pc[up, 0]
            line = jnp.concatenate([line[k:k + 1] for k in range(8)], axis=1)
            total = total + jnp.where(r == (0 if up else rows - 1), line, 0.0)
        gbh[f, HALO:HALO + rows, PAD:PAD + length] = total.astype(BF16)
    for ds in (-1, 1):
        @pl.when(valid(0, ds))
        def _(ds=ds):
            for f in order:
                gb_copy(ds, f).start()

    for pair in pairs[1:]:
        make_beams(pair)

    acc2 = jnp.zeros((3 * TALL3, wide), F32)
    def gram(total, g):
        for h in range(halves):
            total = total + lax.dot_general(
                bs[h, g:g + 3].reshape(3 * TALL3, length), cot_half(g, h),
                (((1,), (1,)), ((), ())), preferred_element_type=F32)
        return total

    for g in range(1, planes - 1):
        acc2 = gram(acc2, g)
    for df in (-1, 1):
        @pl.when(valid(-df, 0))
        def _(df=df):
            bm_copy(df).wait_recv()
    for p in (0, planes + 1):
        spread_beam(p, bm[p].astype(F32))
    for g in (0, planes - 1):
        acc2 = gram(acc2, g)
    lines = []
    for a in range(3):
        for b in range(3):
            for e in range(3):
                tile = acc2[a * TALL3 + e * EDGE:a * TALL3 + (e + 1) * EDGE]
                lines.append(jnp.sum(jnp.where(masks[b], tile, 0.0), axis=0, keepdims=True))
    lines.append(jnp.zeros((128 - 27, wide), F32))
    terms = lax.dot_general(member.astype(F32), jnp.concatenate(lines, axis=0),
                            (((1,), (1,)), ((), ())), precision=lax.Precision.HIGHEST,
                            preferred_element_type=F32)
    half = chans // 2
    packed = terms[:half] + pltpu.roll(terms[half:], 64, 1)
    mine[...] = packed
    slots[si] = packed

    def kg_copy(k, src, dst, send, recv, at, size, axis):
        to = lax.rem(at + k, size)
        return pltpu.make_async_remote_copy(
            src_ref=src, dst_ref=dst.at[at], send_sem=send.at[k], recv_sem=recv.at[k],
            device_id=(to, si) if axis == 0 else (fi, to), device_id_type=MESH)

    def kg_wait(k, src, dst, send, recv, at, size, axis):
        pltpu.make_async_remote_copy(
            src_ref=src, dst_ref=dst.at[lax.rem(at - k + size, size)], send_sem=send.at[k],
            recv_sem=recv.at[k], device_id=(fi, si), device_id_type=MESH).wait_recv()

    over_sky = (mine, slots, s_kg, r_kg, si, ns, 1)
    over_freq = (mine2, slots2, s_kf, r_kf, fi, nf, 0)
    for k in range(1, ns):
        kg_copy(k, *over_sky).start()

    out_copies = [pltpu.make_async_copy(outv.at[f], out_ref.at[f], out_sem.at[f])
                  for f in range(planes)]

    def finish(pair):
        for f, both in zip(pair, blur(gbh, pair)):
            for h in range(halves):
                outv[f, h * HALF:(h + 1) * HALF] = both[h * EDGE:h * EDGE + HALF]
            out_copies[f].start()

    wait_halos(gb_copy, order)
    finish(pairs[0])
    for k in range(1, ns):
        kg_wait(k, *over_sky)
    total = slots[0]
    for k in range(1, ns):
        total = total + slots[k]
    mine2[...] = total
    slots2[fi] = total
    for k in range(1, nf):
        kg_copy(k, *over_freq).start()
    for pair in pairs[1:]:
        finish(pair)
    for k in range(1, nf):
        kg_wait(k, *over_freq)
    total = slots2[0]
    for k in range(1, nf):
        total = total + slots2[k]
    kg_ref[...] = total * scale

    for copy in out_copies:
        copy.wait()
    for i, (df, ds) in enumerate(DIRS):
        @pl.when(valid(df, ds))
        def _(i=i, df=df, ds=ds):
            part_copy(i, df, ds).wait_send()
            if ds == 0:
                bm_copy(df).wait_send()
            if df == 0:
                for f in range(planes):
                    sky_copy(ds, f).wait_send()
                    gb_copy(ds, f).wait_send()
    for k in range(1, ns):
        kg_copy(k, *over_sky).wait_send()
    for k in range(1, nf):
        kg_copy(k, *over_freq).wait_send()


def hand_on(sky_ref, packed_ref, out_ref, kg_ref):
    out_ref[...] = sky_ref[...]

    @pl.when(pl.program_id(0) == 0)
    def _():
        packed = packed_ref[...]
        half = packed.shape[0]
        kg_ref[0:half] = packed[:, :27]
        kg_ref[half:] = pltpu.roll(packed, 64, 1)[:, :27]


def per_device(sky_cube, half_width, conv_weight, out_cotangent):
    planes, rows, length = sky_cube.shape
    chans = conv_weight.shape[0]
    nf, ns = lax.axis_size("freq"), lax.axis_size("sky")
    scale = 1.0 / math.sqrt(planes * nf * rows * ns * length)
    tall = rows + 2 * HALO
    wide = chans * HALF
    halves = rows // HALF
    high = halves * EDGE
    dma = pltpu.SemaphoreType.DMA

    def kernel(*refs):
        body(nf, ns, scale, *refs)

    sky_grad, packed = pl.pallas_call(
        kernel,
        out_shape=(jax.ShapeDtypeStruct((planes, rows, length), F32),
                   jax.ShapeDtypeStruct((chans // 2, 128), F32)),
        in_specs=[pl.BlockSpec(memory_space=pltpu.HBM)] * 4,
        out_specs=(pl.BlockSpec(memory_space=pltpu.HBM), pl.BlockSpec(memory_space=pltpu.VMEM)),
        scratch_shapes=[
            pltpu.VMEM((planes, rows, length), F32), dma((planes,)),
            pltpu.SMEM((planes,), jnp.int32),
            pltpu.VMEM((chans, 27), BF16),
            pltpu.VMEM((planes, tall, length + 2 * PAD), BF16),
            pltpu.VMEM((planes, tall, length + 2 * PAD), BF16),
            pltpu.VMEM((planes, chans, rows, length), BF16),
            pltpu.VMEM((9 * EDGE + 8, wide), BF16),
            pltpu.VMEM((planes + 2, halves, 3, EDGE, length), F32),
            pltpu.VMEM((planes + 2, rows, length), F32),
            pltpu.VMEM((planes + 2, 8, length // 8), F32),
            pltpu.VMEM((planes + 2, 8, length // 8), F32),
            pltpu.VMEM((2, rows, length), F32),
            pltpu.VMEM((2, planes, 8, length // 8), F32),
            pltpu.VMEM((4, 1, 8, length // 8), F32),
            pltpu.VMEM((planes + 2, high, length), BF16),
            pltpu.VMEM((halves, planes + 2, TALL3, length), BF16),
            pltpu.VMEM((planes, 3 * BLOCK, 2 * BLOCK), BF16),
            pltpu.VMEM((planes, 2 * high, 4 * tall), BF16),
            pltpu.VMEM((planes, 8, 256), F32),
            pltpu.VMEM((chans // 2, 128), F32),
            pltpu.VMEM((ns, chans // 2, 128), F32),
            pltpu.VMEM((chans // 2, 128), F32),
            pltpu.VMEM((nf, chans // 2, 128), F32),
            dma((planes,)), dma((3,)),
            dma((2 * planes,)), dma((2 * planes,)), dma((8,)), dma((8,)),
            dma((2 * planes,)), dma((2 * planes,)), dma((2,)), dma((2,)),
            dma((ns,)), dma((ns,)), dma((nf,)), dma((nf,)),
        ],
        compiler_params=pltpu.CompilerParams(
            collective_id=0, has_side_effects=True, vmem_limit_bytes=60 * 1024 * 1024),
        name="beam_backward",
    )(half_width, sky_cube, conv_weight, out_cotangent)
    return pl.pallas_call(
        hand_on,
        out_shape=(jax.ShapeDtypeStruct((planes, rows, length), F32),
                   jax.ShapeDtypeStruct((chans, 27), F32)),
        grid=(planes,),
        in_specs=[pl.BlockSpec((1, rows, length), lambda f: (f, 0, 0)),
                  pl.BlockSpec((chans // 2, 128), lambda f: (0, 0))],
        out_specs=(pl.BlockSpec((1, rows, length), lambda f: (f, 0, 0)),
                   pl.BlockSpec((chans, 27), lambda f: (0, 0))),
        compiler_params=pltpu.CompilerParams(vmem_limit_bytes=60 * 1024 * 1024),
        name="hand_on",
    )(sky_grad, packed)


def solution(mesh):
    return jax.shard_map(
        per_device,
        mesh=mesh,
        in_specs=(P("freq", "sky", None), P("freq"), P(), P(None, "freq", "sky", None)),
        out_specs=(P("freq", "sky", None), P()),
        check_vma=False,
    )
```
